128 devices in a mesh: grp: 4 (over z), elem: 32 (over x, y, core).
Axes of the slice: x: 4, y: 4, z: 4, core: 2. Of those that a mesh axis runs over, the one named last changes fastest.
Arguments:
- velocity: float32 [3, 343, 16384], P(None, None, ('grp', 'elem')), may hold values from -0.6 to 0.6
- adjoint: float32 [3, 343, 16384], P(None, None, ('grp', 'elem')), may hold values from -0.6 to 0.6
- spacing: float32 [3, 16384], P(None, ('grp', 'elem')), may hold values from 0.5 to 2
- elem_count: int32 [128], P(('grp', 'elem')), may hold values from 32 to 128, as said below
- design_map: int32 [8, 16384], P(None, ('grp', 'elem')), may hold values from 0 to 262143, as said below
Outputs:
- direction: float32 [3, 262144], P(None, ('grp', 'elem'))
- objective: float32 [], replicated
The draws below stay inside these ranges and needn't reach their ends.
Inputs may be any that keep to these rules, and one draw needn't show every extreme that they name: `elem_count`: the largest count equals 128 in every draw. `design_map`: design node d belongs to the device numbered d // 2048, counting grp first and elem second. Every entry of a device's columns names a node of a device whose elem index differs from that device's by at most one, cyclically over the elem axis, in any group.
All inputs are finite; a program needn't handle non-finite values.
Results may differ from the reference program's by a relative error of at most 0.0003.
Values sent between devices are 32-bit elements; how exact they have to be, the bound alone decides.
No kernel may reach another device: no remote copies, remote signals or barrier semaphores. Data moves between devices by JAX's collectives and lax.ppermute only.
A program may use at most 64 MiB of HBM per device.

```python
import math
import jax
import jax.numpy as jnp
import numpy as np
from jax import lax

P_SIZE = 7
ELEM_DEV = 128
ND_DEV = 2048
ELEMS = 16384
N_GRP = 4
N_ELEM = 32


def node_field(key, salt):
    elements = ELEM_DEV * N_GRP * N_ELEM
    seeded = jax.random.fold_in(key, salt)
    jitter_key, shared_key = jax.random.split(seeded)
    shared_part = jnp.clip(jax.random.normal(shared_key, (3, P_SIZE ** 3, 1), jnp.float32), -4.0, 4.0)
    jitter_part = jnp.clip(jax.random.normal(jitter_key, (3, P_SIZE ** 3, elements), jnp.float32), -4.0, 4.0)
    return 0.07 * shared_part + 0.07 * jitter_part


def draw_velocity(key, part):
    return node_field(key, 11)


def draw_adjoint(key, part):
    return node_field(key, 23)


def draw_elem_count(key, part):
    devices = N_GRP * N_ELEM
    index = jnp.arange(devices, dtype=jnp.int32)
    base = ELEM_DEV // 3 + index * (ELEM_DEV - ELEM_DEV // 3) // (devices - 1)
    jitter = jax.random.randint(key, (devices,), 0, max(ELEM_DEV // 16, 2), dtype=jnp.int32)
    jitter = jnp.where(index == devices - 1, 0, jitter)
    return (base - jitter).astype(jnp.int32)


def draw_design_map(key, part):
    devices = N_GRP * N_ELEM
    total = ELEM_DEV * devices
    column = jnp.arange(total, dtype=jnp.int32)
    device = column // ELEM_DEV
    home_grp = (device // N_ELEM)[None, :]
    home_col = (device % N_ELEM)[None, :]
    first, second, third, fourth = jax.random.split(key, 4)
    same = jax.random.randint(first, (8, total), 0, 2, dtype=jnp.int32)
    other = jax.random.randint(second, (8, total), 1, N_GRP, dtype=jnp.int32)
    owner_grp = jnp.where(same == 1, home_grp, (home_grp + other) % N_GRP)
    offset = jax.random.randint(third, (8, total), -1, 2, dtype=jnp.int32)
    owner_col = (home_col + offset + N_ELEM) % N_ELEM
    vertex_ids = jnp.arange(8, dtype=jnp.int32)[:, None]
    within = 8 * jax.random.randint(fourth, (8, total), 0, ND_DEV // 8, dtype=jnp.int32) + vertex_ids
    return ((owner_grp * N_ELEM + owner_col) * ND_DEV + within).astype(jnp.int32)


def levels(stream_key, shape, cuts, low, top_value):
    factor_of = 1.0
    for position, blocks in cuts:
        draws = jax.random.uniform(jax.random.fold_in(jax.random.fold_in(stream_key, 6), position), (blocks,), jnp.float32, low / len(cuts), top_value / len(cuts))
        factor_of = factor_of * jnp.repeat(jnp.exp(draws), shape[position] // blocks).reshape((-1,) + (1,) * (len(shape) - 1 - position))
    return factor_of


def setup_inputs(seed: int = 0) -> dict:
    keys = jax.random.split(jax.random.key(seed), 6)
    velocity = draw_velocity(jax.random.fold_in(keys[5], 71), 0)
    adjoint = draw_adjoint(jax.random.fold_in(keys[5], 71), 0)
    spacing = jnp.clip(jnp.exp(math.log(2.0) - 1.3862944 * jax.random.uniform(keys[2], (3, ELEMS), jnp.float32) ** levels(keys[2], (3, ELEMS), ((1, 128),), -0.2, 0.2)), 0.5, 2.0)
    elem_count = draw_elem_count(jax.random.fold_in(keys[5], 71), 0)
    design_map = draw_design_map(jax.random.fold_in(keys[5], 71), 0)
    return {"velocity": velocity, "adjoint": adjoint, "spacing": spacing, "elem_count": elem_count, "design_map": design_map}


def lobatto(degree):
    points = np.cos(np.pi * np.arange(degree + 1) / degree)
    for sweep in range(60):
        lower = np.ones(degree + 1)
        upper = points.copy()
        for order in range(2, degree + 1):
            lower, upper = (upper, ((2 * order - 1) * points * upper - (order - 1) * lower) / order)
        points = points - (points * upper - lower) / ((degree + 1) * upper)
    lower = np.ones(degree + 1)
    upper = points.copy()
    for order in range(2, degree + 1):
        lower, upper = (upper, ((2 * order - 1) * points * upper - (order - 1) * lower) / order)
    return (points[::-1].copy(), upper[::-1].copy())

def tables():
    degree = P_SIZE - 1
    points, values = lobatto(degree)
    weights = 2.0 / (degree * (degree + 1) * values ** 2)
    derivative = np.zeros((P_SIZE, P_SIZE))
    for i in range(P_SIZE):
        for j in range(P_SIZE):
            if i != j:
                derivative[i, j] = values[i] / (values[j] * (points[i] - points[j]))
    derivative[0, 0] = -degree * (degree + 1) / 4.0
    derivative[P_SIZE - 1, P_SIZE - 1] = degree * (degree + 1) / 4.0
    coords = np.meshgrid(points, points, points, indexing='ij')
    coords = [c.reshape(-1) for c in coords]
    spread = np.meshgrid(weights, weights, weights, indexing='ij')
    quadrature = (spread[0] * spread[1] * spread[2]).reshape(-1)
    vertex_grad = np.zeros((3, 8, P_SIZE ** 3))
    for vertex in range(8):
        signs = [2.0 * (vertex >> 2 - m & 1) - 1.0 for m in range(3)]
        factors = [(1.0 + signs[m] * coords[m]) / 2.0 for m in range(3)]
        for j in range(3):
            others = [factors[m] for m in range(3) if m != j]
            vertex_grad[j, vertex] = signs[j] / 2.0 * others[0] * others[1] * quadrature
    return (jnp.asarray(derivative, jnp.float32), jnp.asarray(vertex_grad, jnp.float32), jnp.asarray(quadrature, jnp.float32))

def element_terms(velocity, adjoint, spacing, derivative, vertex_grad, quadrature):
    blocks = velocity.shape[-1]
    factor = 2.0 / spacing
    jacobian = spacing[0] * spacing[1] * spacing[2] / 8.0
    highest = lax.Precision.HIGHEST

    def gradient(field):
        cube = field.reshape(3, P_SIZE, P_SIZE, P_SIZE, blocks)
        first = jnp.einsum('ij,cjklb->ciklb', derivative, cube, precision=highest)
        second = jnp.einsum('ij,ckjlb->ckilb', derivative, cube, precision=highest)
        third = jnp.einsum('ij,ckljb->cklib', derivative, cube, precision=highest)
        stacked = jnp.stack([first, second, third], axis=1).reshape(3, 3, P_SIZE ** 3, blocks)
        return stacked * factor[None, :, None, :]
    grad_u = gradient(velocity)
    grad_w = gradient(adjoint)
    inner = lax.optimization_barrier(jnp.sum(grad_u * grad_w, axis=(0, 1)))
    cross = jnp.einsum('icqb,ijqb->cjqb', grad_u, grad_w, precision=highest)
    unit = jnp.eye(3, dtype=jnp.float32)
    stress = unit[:, :, None, None] * inner[None, None] - cross - jnp.swapaxes(cross, 0, 1)
    contrib = jnp.einsum('cjqb,jkq->cjkb', stress, vertex_grad, precision=highest)
    terms = lax.optimization_barrier(jnp.sum(contrib * factor[None, :, None, :], axis=1)) * jacobian[None, None, :]
    squared = lax.optimization_barrier(jnp.sum(grad_u * grad_u, axis=(0, 1)))
    dissipated = jacobian * jnp.einsum('qb,q->b', squared, quadrature, precision=highest)
    return (terms, dissipated)

def reference(velocity, adjoint, spacing, elem_count, design_map):
    devices = N_GRP * N_ELEM
    design_total = ND_DEV * devices
    derivative, vertex_grad, quadrature = tables()

    def one_device(carry, device):
        gradient_sum, spent = carry
        start = (device * ELEM_DEV).astype(jnp.int32)
        field_u = lax.dynamic_slice_in_dim(velocity, start, ELEM_DEV, 2)
        field_w = lax.dynamic_slice_in_dim(adjoint, start, ELEM_DEV, 2)
        lengths = lax.dynamic_slice_in_dim(spacing, start, ELEM_DEV, 1)
        nodes = lax.dynamic_slice_in_dim(design_map, start, ELEM_DEV, 1)
        terms, dissipated = element_terms(field_u, field_w, lengths, derivative, vertex_grad, quadrature)
        live = (jnp.arange(ELEM_DEV, dtype=jnp.int32) < elem_count[device]).astype(jnp.float32)
        terms = terms * live[None, None, :]
        gradient_sum = gradient_sum.at[:, nodes.reshape(-1)].add(terms.reshape(3, -1))
        return ((gradient_sum, spent + jnp.sum(dissipated * live)), None)
    init = (jnp.zeros((3, design_total), jnp.float32), jnp.zeros((), jnp.float32))
    (gradient_sum, spent), _ = lax.scan(one_device, init, jnp.arange(devices, dtype=jnp.int32))
    mean_square = jnp.sum(gradient_sum * gradient_sum) / (3.0 * design_total)
    direction = gradient_sum * lax.rsqrt(mean_square + 1e-06)
    objective = spent / (P_SIZE ** 3 * ELEM_DEV * devices)
    return (direction, objective)
```

```python
import functools

import jax
import jax.numpy as jnp
import numpy as np
from jax import lax
from jax.experimental import pallas as pl
from jax.experimental.pallas import tpu as pltpu
from jax.sharding import Mesh
from jax.sharding import PartitionSpec as P

P_SIZE = 7
NODES = P_SIZE**3
ND_DEV = 2048
LANES = 128
ELEM = ("elem_0", "elem_1", "elem_2")
GRP_ELEM = ("grp", "elem_0", "elem_1", "elem_2")
SENT = 40
WIDE = 256


def lobatto(degree):
    points = np.cos(np.pi * np.arange(degree + 1) / degree)
    for sweep in range(60):
        lower = np.ones(degree + 1)
        upper = points.copy()
        for order in range(2, degree + 1):
            lower, upper = (upper, ((2 * order - 1) * points * upper - (order - 1) * lower) / order)
        points = points - (points * upper - lower) / ((degree + 1) * upper)
    lower = np.ones(degree + 1)
    upper = points.copy()
    for order in range(2, degree + 1):
        lower, upper = (upper, ((2 * order - 1) * points * upper - (order - 1) * lower) / order)
    return (points[::-1].copy(), upper[::-1].copy())


def one_dimensional():
    degree = P_SIZE - 1
    points, values = lobatto(degree)
    weights = 2.0 / (degree * (degree + 1) * values**2)
    derivative = np.zeros((P_SIZE, P_SIZE))
    for i in range(P_SIZE):
        for j in range(P_SIZE):
            if i != j:
                derivative[i, j] = values[i] / (values[j] * (points[i] - points[j]))
    derivative[0, 0] = -degree * (degree + 1) / 4.0
    derivative[degree, degree] = degree * (degree + 1) / 4.0
    points[degree // 2] = 0.0
    derivative[degree // 2, degree // 2] = 0.0
    return (points, weights, derivative)


POINTS, WEIGHTS, DERIVATIVE = one_dimensional()
COLUMN, ACROSS, ALONG, SIGNS = 0, 56, 72, 88
TABLE_ROWS = 144


def table():
    rows = np.zeros((TABLE_ROWS, LANES), np.float32)
    for c in range(P_SIZE):
        rows[COLUMN + 8 * c : COLUMN + 8 * c + P_SIZE] = DERIVATIVE[:, c][:, None]
    rows[ACROSS : ACROSS + P_SIZE] = WEIGHTS[:, None]
    rows[ACROSS + 8 : ACROSS + 8 + P_SIZE] = (WEIGHTS * POINTS)[:, None]
    rows[ALONG : ALONG + P_SIZE] = WEIGHTS[:, None]
    rows[ALONG + 8 : ALONG + 8 + P_SIZE] = (WEIGHTS * POINTS)[:, None]
    for number, axes in enumerate(((0,), (1,), (2,), (0, 1), (0, 2), (1, 2), (0, 1, 2))):
        for vertex in range(8):
            sign = np.prod([2.0 * (vertex >> 2 - m & 1) - 1.0 for m in axes])
            rows[SIGNS + 8 * number + vertex] = sign / 8.0
    return rows


def along_vectors(f):
    half = P_SIZE // 2
    last = P_SIZE - 1
    even = [f[j] + f[last - j] for j in range(half)]
    odd = [f[j] - f[last - j] for j in range(half)]
    out = [None] * P_SIZE
    for i in range(half + 1):
        coef = DERIVATIVE[i]
        b = None
        for j in range(half):
            piece = float((coef[j] - coef[last - j]) / 2) * odd[j]
            b = piece if b is None else b + piece
        if i == half:
            out[i] = b
            continue
        a = float(coef[half]) * f[half]
        for j in range(half):
            a = a + float((coef[j] + coef[last - j]) / 2) * even[j]
        out[i] = b + a
        out[last - i] = b - a
    return out


def terms_kernel(count_ref, u_ref, w_ref, h_ref, map_ref, tab_ref, out_ref, ga_ref, gb_ref, mom_ref):
    n = P_SIZE
    fields = [(ref, i) for ref in (u_ref, w_ref) for i in range(3)]
    rows = pl.ds(0, n)

    def first(b, carry):
        for f, (ref, i) in enumerate(fields):
            slabs = [ref[i, pl.ds(a * n * n + b * n, n), :] for a in range(n)]
            for a, value in enumerate(along_vectors(slabs)):
                ga_ref[f, a, b, rows, :] = value
        return carry

    lax.fori_loop(0, n, first, 0)
    mom_ref[...] = jnp.zeros_like(mom_ref)

    h = h_ref[...]
    factor = [2.0 / h[j : j + 1] for j in range(3)]
    square = [f * f for f in factor]

    def second(a, carry):
        base = a * n * n
        for f, (ref, i) in enumerate(fields):
            slabs = [ref[i, pl.ds(base + b * n, n), :] for b in range(n)]
            for b, value in enumerate(along_vectors(slabs)):
                gb_ref[f, b, rows, :] = value
        sums = [[None, None] for _ in range(6)]
        spent = None
        for b in range(n):
            grads = []
            for f, (ref, i) in enumerate(fields):
                gc = None
                for c in range(n):
                    row = ref[i, pl.ds(base + b * n + c, 1), :]
                    piece = tab_ref[pl.ds(COLUMN + 8 * c, n), :] * row
                    gc = piece if gc is None else gc + piece
                grads.append([ga_ref[f, a, b, rows, :], gb_ref[f, b, rows, :], gc])
            gu, gw = grads[:3], grads[3:]

            def cross(c, j):
                return gu[0][c] * gw[0][j] + gu[1][c] * gw[1][j] + gu[2][c] * gw[2][j]

            pairs = [cross(0, 0), cross(1, 1), cross(2, 2)]
            pairs += [cross(c, j) + cross(j, c) for c, j in ((0, 1), (0, 2), (1, 2))]
            own = [gu[0][j] * gu[0][j] + gu[1][j] * gu[1][j] + gu[2][j] * gu[2][j] for j in range(3)]
            squared = own[0] * square[0] + own[1] * square[1] + own[2] * square[2]
            weight = float(WEIGHTS[b])
            slope = float(WEIGHTS[b] * POINTS[b])
            for s, value in enumerate(pairs):
                piece = weight * value
                sums[s][0] = piece if sums[s][0] is None else sums[s][0] + piece
                if b != n // 2:
                    piece = slope * value
                    sums[s][1] = piece if sums[s][1] is None else sums[s][1] + piece
            piece = weight * squared
            spent = piece if spent is None else spent + piece
        wa = tab_ref[pl.ds(ALONG + a, 1), :]
        wxa = tab_ref[pl.ds(ALONG + 8 + a, 1), :]
        for s in range(6):
            for r, scale in enumerate((wa, wxa)):
                for t in range(2):
                    at = s * 4 + r * 2 + t
                    mom_ref[at, rows, :] = mom_ref[at, rows, :] + scale * sums[s][t]
        mom_ref[24, rows, :] = mom_ref[24, rows, :] + wa * spent
        return carry

    lax.fori_loop(0, n, second, 0)

    jacobian = h[0:1] * h[1:2] * h[2:3] * 0.125
    lanes = lax.broadcasted_iota(jnp.int32, (1, LANES), 1)
    live = jacobian * (lanes < count_ref[0]).astype(jnp.float32)
    flat = tab_ref[pl.ds(ACROSS, n), :]
    slant = tab_ref[pl.ds(ACROSS + 8, n), :]
    signs = [tab_ref[pl.ds(SIGNS + 8 * i, 8), :] for i in range(7)]

    def moment(value, c):
        return jnp.sum(value * (slant if c else flat), axis=0, keepdims=True)

    def along(axis, part):
        others = [m for m in range(3) if m != axis]
        total = None
        for low in range(2):
            for high in range(2):
                powers = [0, 0, 0]
                powers[others[0]] = low
                powers[others[1]] = high
                axes = tuple(sorted([axis] + [m for m in others if powers[m]]))
                number = {(0,): 0, (1,): 1, (2,): 2, (0, 1): 3, (0, 2): 4, (1, 2): 5, (0, 1, 2): 6}[axes]
                piece = signs[number] * moment(part[powers[0] * 2 + powers[1]], powers[2])
                total = piece if total is None else total + piece
        return total

    mom = [[mom_ref[s * 4 + i, rows, :] for i in range(4)] for s in range(6)]
    inner = [
        square[0] * mom[0][i] + square[1] * mom[1][i] + square[2] * mom[2][i] for i in range(4)
    ]
    between = {(0, 1): 3, (0, 2): 4, (1, 2): 5}
    for c in range(3):
        part = [inner[i] - (2.0 * square[c]) * mom[c][i] for i in range(4)]
        total = along(c, part)
        for j in range(3):
            if j != c:
                shared = mom[between[(min(c, j), max(c, j))]]
                total = total - square[j] * along(j, shared)
        out_ref[pl.ds(8 * c, 8), :] = total * (factor[c] * live)
    out_ref[pl.ds(24, 8), :] = map_ref[...].astype(jnp.float32)
    spent = live * moment(mom_ref[24, rows, :], 0)
    out_ref[pl.ds(32, 8), :] = jnp.broadcast_to(spent, (8, LANES))


def element_terms(count, velocity, adjoint, spacing, design_map):
    vmem = pl.BlockSpec(memory_space=pltpu.VMEM)
    return pl.pallas_call(
        terms_kernel,
        out_shape=jax.ShapeDtypeStruct((SENT, LANES), jnp.float32),
        in_specs=[pl.BlockSpec(memory_space=pltpu.SMEM)] + [vmem] * 5,
        out_specs=vmem,
        scratch_shapes=[
            pltpu.VMEM((6, P_SIZE, P_SIZE, 8, LANES), jnp.float32),
            pltpu.VMEM((6, P_SIZE, 8, LANES), jnp.float32),
            pltpu.VMEM((25, 8, LANES), jnp.float32),
        ],
        compiler_params=pltpu.CompilerParams(vmem_limit_bytes=32 * 1024 * 1024),
    )(count, velocity, adjoint, spacing, design_map, jnp.asarray(table()))


def assemble_kernel(groups, columns, place_ref, own_ref, *refs):
    others = refs[: groups - 1]
    grad_ref, part_ref, left_ref, right_ref, sum_ref = refs[groups - 1 :]
    group = place_ref[0]
    column = place_ref[1]
    per_owner = ND_DEV // WIDE
    high = groups * per_owner
    iota_wide = lax.broadcasted_iota(jnp.int32, (WIDE, LANES), 0)
    iota_high = lax.broadcasted_iota(jnp.int32, (high, LANES), 0)
    sum_ref[...] = jnp.zeros_like(sum_ref)
    for source in (own_ref, *others):

        def add(s, carry):
            for k in range(8):
                node = source[s, pl.ds(24 + k, 1), :].astype(jnp.int32)
                owner = node // ND_DEV
                mine = owner % columns == column
                low = node % WIDE
                at = (owner // columns) * per_owner + (node % ND_DEV) // WIDE
                at = jnp.where(mine, at, -1)
                lanes = pl.ds(k * LANES, LANES)
                right_ref[:, lanes] = jnp.where(iota_wide == low, 1.0, 0.0).astype(jnp.bfloat16)
                hit = iota_high == at
                for c in range(3):
                    value = source[s, pl.ds(8 * c + k, 1), :]
                    coarse = value.astype(jnp.bfloat16).astype(jnp.float32)
                    for piece, part in enumerate((coarse, value - coarse)):
                        row = (piece * 3 + c) * high
                        left_ref[pl.ds(row, high), lanes] = jnp.where(hit, part, 0.0).astype(
                            jnp.bfloat16
                        )
            sum_ref[...] += lax.dot_general(
                left_ref[...],
                right_ref[...],
                (((1,), (1,)), ((), ())),
                preferred_element_type=jnp.float32,
            )
            return carry

        lax.fori_loop(0, 3, add, 0)
    total = sum_ref[pl.ds(0, 3 * high), :] + sum_ref[pl.ds(3 * high, 3 * high), :]
    squares = jnp.sum(total * total)
    sum_ref[pl.ds(0, 3 * high), :] = total
    for c in range(3):
        block = sum_ref[pl.ds(c * high + group * per_owner, per_owner), :]
        for i in range(per_owner):
            grad_ref[c : c + 1, i * WIDE : (i + 1) * WIDE] = block[i : i + 1, :]
    spent = own_ref[0, pl.ds(32, 1), :]
    for other in others:
        spent = spent + other[0, pl.ds(32, 1), :]
    spent = jnp.sum(spent)
    lane = lax.broadcasted_iota(jnp.int32, (1, LANES), 1)
    stats = jnp.where(lane == 0, squares, jnp.where(lane == 1, spent, 0.0))
    part_ref[...] = jnp.broadcast_to(stats[None], part_ref.shape)


def assembled(place, arrays, columns):
    groups = len(arrays)
    high = groups * (ND_DEV // WIDE)
    vmem = pl.BlockSpec(memory_space=pltpu.VMEM)
    return pl.pallas_call(
        functools.partial(assemble_kernel, groups, columns),
        out_shape=(
            jax.ShapeDtypeStruct((3, ND_DEV), jnp.float32),
            jax.ShapeDtypeStruct((columns, 1, LANES), jnp.float32),
        ),
        in_specs=[pl.BlockSpec(memory_space=pltpu.SMEM)] + [vmem] * groups,
        out_specs=(vmem, vmem),
        scratch_shapes=[
            pltpu.VMEM((6 * high, 8 * LANES), jnp.bfloat16),
            pltpu.VMEM((WIDE, 8 * LANES), jnp.bfloat16),
            pltpu.VMEM((6 * high, WIDE), jnp.float32),
        ],
        compiler_params=pltpu.CompilerParams(vmem_limit_bytes=32 * 1024 * 1024),
    )(place, *arrays)


def scale_kernel(over_nodes, over_elements, grad_ref, part_ref, out_ref, objective_ref):
    total = jnp.sum(part_ref[:, 0, :], axis=0, keepdims=True)
    lane = lax.broadcasted_iota(jnp.int32, (1, LANES), 1)
    squares = jnp.sum(jnp.where(lane == 0, total, 0.0), axis=1, keepdims=True)
    spent = jnp.sum(jnp.where(lane == 1, total, 0.0), axis=1, keepdims=True)
    out_ref[...] = grad_ref[...] * lax.rsqrt(squares * over_nodes + 1e-06)
    objective_ref[...] = spent * over_elements


def scaled(grad, parts, over_nodes, over_elements):
    vmem = pl.BlockSpec(memory_space=pltpu.VMEM)
    return pl.pallas_call(
        functools.partial(scale_kernel, over_nodes, over_elements),
        out_shape=(
            jax.ShapeDtypeStruct((3, ND_DEV), jnp.float32),
            jax.ShapeDtypeStruct((1, 1), jnp.float32),
        ),
        in_specs=[vmem, vmem],
        out_specs=(vmem, vmem),
    )(grad, parts)


def shifted(array, axis, by):
    devices = lax.axis_size(axis)
    return lax.ppermute(array, axis, [(i, (i + by) % devices) for i in range(devices)])


def body(velocity, adjoint, spacing, elem_count, design_map):
    slots = velocity.shape[-1]
    groups = lax.axis_size("grp")
    columns = lax.axis_size(ELEM)
    sent = element_terms(elem_count, velocity, adjoint, spacing, design_map)
    within = lax.ppermute(sent, "elem_2", [(0, 1), (1, 0)])
    partner = [(e + 1) % columns if e % 2 else (e - 1) % columns for e in range(columns)]
    across = lax.ppermute(sent, ELEM, list(enumerate(partner)))
    three = jnp.stack([sent, within, across])
    arrays = [three] + [shifted(three, "grp", by) for by in range(1, groups)]
    place = jnp.stack([lax.axis_index("grp"), lax.axis_index(ELEM)]).astype(jnp.int32)
    grad, parts = assembled(place, arrays, columns)
    parts = lax.all_to_all(parts, ELEM, split_axis=0, concat_axis=0, tiled=True)
    devices = groups * columns
    direction, objective = scaled(
        grad,
        parts,
        1.0 / (3.0 * ND_DEV * devices),
        1.0 / (NODES * slots * devices),
    )
    return (direction, objective.reshape(()))


def solution(mesh):
    finer = Mesh(
        mesh.devices.reshape(mesh.shape["grp"], 4, 4, 2), ("grp", "elem_0", "elem_1", "elem_2")
    )
    in_specs = (
        P(None, None, GRP_ELEM),
        P(None, None, GRP_ELEM),
        P(None, GRP_ELEM),
        P(GRP_ELEM),
        P(None, GRP_ELEM),
    )
    out_specs = (P(None, GRP_ELEM), P())
    return jax.shard_map(body, mesh=finer, in_specs=in_specs, out_specs=out_specs, check_vma=False)
```

```python
import functools

import jax
import jax.numpy as jnp
import numpy as np
from jax import lax
from jax.experimental import pallas as pl
from jax.experimental.pallas import tpu as pltpu
from jax.sharding import Mesh
from jax.sharding import PartitionSpec as P

P_SIZE = 7
NODES = P_SIZE**3
ND_DEV = 2048
LANES = 128
ELEM = ("elem_0", "elem_1", "elem_2")
GRP_ELEM = ("grp", "elem_0", "elem_1", "elem_2")
SENT = 40
WIDE = 256


def lobatto(degree):
    points = np.cos(np.pi * np.arange(degree + 1) / degree)
    for sweep in range(60):
        lower = np.ones(degree + 1)
        upper = points.copy()
        for order in range(2, degree + 1):
            lower, upper = (upper, ((2 * order - 1) * points * upper - (order - 1) * lower) / order)
        points = points - (points * upper - lower) / ((degree + 1) * upper)
    lower = np.ones(degree + 1)
    upper = points.copy()
    for order in range(2, degree + 1):
        lower, upper = (upper, ((2 * order - 1) * points * upper - (order - 1) * lower) / order)
    return (points[::-1].copy(), upper[::-1].copy())


def one_dimensional():
    degree = P_SIZE - 1
    points, values = lobatto(degree)
    weights = 2.0 / (degree * (degree + 1) * values**2)
    derivative = np.zeros((P_SIZE, P_SIZE))
    for i in range(P_SIZE):
        for j in range(P_SIZE):
            if i != j:
                derivative[i, j] = values[i] / (values[j] * (points[i] - points[j]))
    derivative[0, 0] = -degree * (degree + 1) / 4.0
    derivative[degree, degree] = degree * (degree + 1) / 4.0
    points[degree // 2] = 0.0
    derivative[degree // 2, degree // 2] = 0.0
    return (points, weights, derivative)


POINTS, WEIGHTS, DERIVATIVE = one_dimensional()
COLUMN, ACROSS, ALONG, SIGNS = 0, 56, 72, 88
TABLE_ROWS = 144


def table():
    rows = np.zeros((TABLE_ROWS, LANES), np.float32)
    for c in range(P_SIZE):
        rows[COLUMN + 8 * c : COLUMN + 8 * c + P_SIZE] = DERIVATIVE[:, c][:, None]
    rows[ACROSS : ACROSS + P_SIZE] = WEIGHTS[:, None]
    rows[ACROSS + 8 : ACROSS + 8 + P_SIZE] = (WEIGHTS * POINTS)[:, None]
    rows[ALONG : ALONG + P_SIZE] = WEIGHTS[:, None]
    rows[ALONG + 8 : ALONG + 8 + P_SIZE] = (WEIGHTS * POINTS)[:, None]
    for number, axes in enumerate(((0,), (1,), (2,), (0, 1), (0, 2), (1, 2), (0, 1, 2))):
        for vertex in range(8):
            sign = np.prod([2.0 * (vertex >> 2 - m & 1) - 1.0 for m in axes])
            rows[SIGNS + 8 * number + vertex] = sign / 8.0
    return rows


def along_vectors(f):
    half = P_SIZE // 2
    last = P_SIZE - 1
    even = [f[j] + f[last - j] for j in range(half)]
    odd = [f[j] - f[last - j] for j in range(half)]
    out = [None] * P_SIZE
    for i in range(half + 1):
        coef = DERIVATIVE[i]
        b = None
        for j in range(half):
            piece = float((coef[j] - coef[last - j]) / 2) * odd[j]
            b = piece if b is None else b + piece
        if i == half:
            out[i] = b
            continue
        a = float(coef[half]) * f[half]
        for j in range(half):
            a = a + float((coef[j] + coef[last - j]) / 2) * even[j]
        out[i] = b + a
        out[last - i] = b - a
    return out


def terms_kernel(
    count_ref,
    u_hbm,
    w_hbm,
    h_hbm,
    map_hbm,
    tab_hbm,
    out_ref,
    u_ref,
    w_ref,
    h_ref,
    map_ref,
    tab_ref,
    ga_ref,
    gb_ref,
    mom_ref,
    sems,
):
    n = P_SIZE
    fields = [(ref, i) for ref in (u_ref, w_ref) for i in range(3)]
    rows = pl.ds(0, n)
    pairs = (
        (u_hbm, u_ref),
        (w_hbm, w_ref),
        (tab_hbm, tab_ref),
        (h_hbm, h_ref),
        (map_hbm, map_ref),
    )
    copies = [
        pltpu.make_async_copy(source, target, sems.at[i])
        for i, (source, target) in enumerate(pairs)
    ]
    for copy in copies:
        copy.start()

    def first(f, ref, i, b):
        slabs = [ref[i, pl.ds(a * n * n + b * n, n), :] for a in range(n)]
        for a, value in enumerate(along_vectors(slabs)):
            ga_ref[f, a, b, rows, :] = value

    def half(start):
        def step(b, carry):
            for f in range(start, start + 3):
                first(f, *fields[f], b)
            return carry

        lax.fori_loop(0, n, step, 0)

    mom_ref[...] = jnp.zeros_like(mom_ref)
    copies[0].wait()
    half(0)
    copies[1].wait()
    half(3)
    for copy in copies[2:]:
        copy.wait()

    h = h_ref[...]
    factor = [2.0 / h[j : j + 1] for j in range(3)]
    square = [f * f for f in factor]

    def second(a, carry):
        base = a * n * n
        for f, (ref, i) in enumerate(fields):
            slabs = [ref[i, pl.ds(base + b * n, n), :] for b in range(n)]
            for b, value in enumerate(along_vectors(slabs)):
                gb_ref[f, b, rows, :] = value
        sums = [[None, None] for _ in range(6)]
        spent = None
        for b in range(n):
            grads = []
            for f, (ref, i) in enumerate(fields):
                gc = None
                for c in range(n):
                    row = ref[i, pl.ds(base + b * n + c, 1), :]
                    piece = tab_ref[pl.ds(COLUMN + 8 * c, n), :] * row
                    gc = piece if gc is None else gc + piece
                grads.append([ga_ref[f, a, b, rows, :], gb_ref[f, b, rows, :], gc])
            gu, gw = grads[:3], grads[3:]

            def cross(c, j):
                return gu[0][c] * gw[0][j] + gu[1][c] * gw[1][j] + gu[2][c] * gw[2][j]

            pairs = [cross(0, 0), cross(1, 1), cross(2, 2)]
            pairs += [cross(c, j) + cross(j, c) for c, j in ((0, 1), (0, 2), (1, 2))]
            own = [gu[0][j] * gu[0][j] + gu[1][j] * gu[1][j] + gu[2][j] * gu[2][j] for j in range(3)]
            squared = own[0] * square[0] + own[1] * square[1] + own[2] * square[2]
            weight = float(WEIGHTS[b])
            slope = float(WEIGHTS[b] * POINTS[b])
            for s, value in enumerate(pairs):
                piece = weight * value
                sums[s][0] = piece if sums[s][0] is None else sums[s][0] + piece
                if b != n // 2:
                    piece = slope * value
                    sums[s][1] = piece if sums[s][1] is None else sums[s][1] + piece
            piece = weight * squared
            spent = piece if spent is None else spent + piece
        wa = tab_ref[pl.ds(ALONG + a, 1), :]
        wxa = tab_ref[pl.ds(ALONG + 8 + a, 1), :]
        for s in range(6):
            for r, scale in enumerate((wa, wxa)):
                for t in range(2):
                    at = s * 4 + r * 2 + t
                    mom_ref[at, rows, :] = mom_ref[at, rows, :] + scale * sums[s][t]
        mom_ref[24, rows, :] = mom_ref[24, rows, :] + wa * spent
        return carry

    lax.fori_loop(0, n, second, 0)

    jacobian = h[0:1] * h[1:2] * h[2:3] * 0.125
    lanes = lax.broadcasted_iota(jnp.int32, (1, LANES), 1)
    live = jacobian * (lanes < count_ref[0]).astype(jnp.float32)
    flat = tab_ref[pl.ds(ACROSS, n), :]
    slant = tab_ref[pl.ds(ACROSS + 8, n), :]
    signs = [tab_ref[pl.ds(SIGNS + 8 * i, 8), :] for i in range(7)]

    def moment(value, c):
        return jnp.sum(value * (slant if c else flat), axis=0, keepdims=True)

    def along(axis, part):
        others = [m for m in range(3) if m != axis]
        total = None
        for low in range(2):
            for high in range(2):
                powers = [0, 0, 0]
                powers[others[0]] = low
                powers[others[1]] = high
                axes = tuple(sorted([axis] + [m for m in others if powers[m]]))
                number = {(0,): 0, (1,): 1, (2,): 2, (0, 1): 3, (0, 2): 4, (1, 2): 5, (0, 1, 2): 6}[axes]
                piece = signs[number] * moment(part[powers[0] * 2 + powers[1]], powers[2])
                total = piece if total is None else total + piece
        return total

    mom = [[mom_ref[s * 4 + i, rows, :] for i in range(4)] for s in range(6)]
    inner = [
        square[0] * mom[0][i] + square[1] * mom[1][i] + square[2] * mom[2][i] for i in range(4)
    ]
    between = {(0, 1): 3, (0, 2): 4, (1, 2): 5}
    for c in range(3):
        part = [inner[i] - (2.0 * square[c]) * mom[c][i] for i in range(4)]
        total = along(c, part)
        for j in range(3):
            if j != c:
                shared = mom[between[(min(c, j), max(c, j))]]
                total = total - square[j] * along(j, shared)
        out_ref[pl.ds(8 * c, 8), :] = total * (factor[c] * live)
    out_ref[pl.ds(24, 8), :] = map_ref[...].astype(jnp.float32)
    spent = live * moment(mom_ref[24, rows, :], 0)
    out_ref[pl.ds(32, 8), :] = jnp.broadcast_to(spent, (8, LANES))


def element_terms(count, velocity, adjoint, spacing, design_map):
    vmem = pl.BlockSpec(memory_space=pltpu.VMEM)
    arrays = (velocity, adjoint, spacing, design_map, jnp.asarray(table()))
    arrays = [pltpu.with_memory_space_constraint(array, pltpu.HBM) for array in arrays]
    return pl.pallas_call(
        terms_kernel,
        out_shape=pltpu.VMEM((SENT, LANES), jnp.float32),
        in_specs=[pl.BlockSpec(memory_space=pltpu.SMEM)]
        + [pl.BlockSpec(memory_space=pltpu.HBM)] * 5,
        out_specs=vmem,
        scratch_shapes=[
            pltpu.VMEM(velocity.shape, jnp.float32),
            pltpu.VMEM(adjoint.shape, jnp.float32),
            pltpu.VMEM(spacing.shape, jnp.float32),
            pltpu.VMEM(design_map.shape, jnp.int32),
            pltpu.VMEM((TABLE_ROWS, LANES), jnp.float32),
            pltpu.VMEM((6, P_SIZE, P_SIZE, 8, LANES), jnp.float32),
            pltpu.VMEM((6, P_SIZE, 8, LANES), jnp.float32),
            pltpu.VMEM((25, 8, LANES), jnp.float32),
            pltpu.SemaphoreType.DMA((5,)),
        ],
        compiler_params=pltpu.CompilerParams(vmem_limit_bytes=16 * 1024 * 1024),
    )(count, *arrays)


def spread_kernel(groups, columns, adds, column_ref, source, *refs):
    base_ref = refs[0] if adds else None
    sum_ref, left_ref, right_ref = refs[-3:]
    column = column_ref[0]
    per_owner = ND_DEV // WIDE
    high = groups * per_owner
    iota_wide = lax.broadcasted_iota(jnp.int32, (WIDE, LANES), 0)
    iota_high = lax.broadcasted_iota(jnp.int32, (high, LANES), 0)
    for k in range(8):
        node = source[pl.ds(24 + k, 1), :].astype(jnp.int32)
        owner = node // ND_DEV
        mine = owner % columns == column
        low = node % WIDE
        at = (owner // columns) * per_owner + (node % ND_DEV) // WIDE
        at = jnp.where(mine, at, -1)
        lanes = pl.ds(k * LANES, LANES)
        right_ref[:, lanes] = jnp.where(iota_wide == low, 1.0, 0.0).astype(jnp.bfloat16)
        hit = iota_high == at
        for c in range(3):
            value = source[pl.ds(8 * c + k, 1), :]
            coarse = value.astype(jnp.bfloat16).astype(jnp.float32)
            for piece, part in enumerate((coarse, value - coarse)):
                row = (piece * 3 + c) * high
                left_ref[pl.ds(row, high), lanes] = jnp.where(hit, part, 0.0).astype(jnp.bfloat16)
    both = lax.dot_general(
        left_ref[...],
        right_ref[...],
        (((1,), (1,)), ((), ())),
        preferred_element_type=jnp.float32,
    )
    total = both[: 3 * high] + both[3 * high :]
    rest = pl.ds(3 * high, 8)
    if adds:
        sum_ref[pl.ds(0, 3 * high), :] = base_ref[pl.ds(0, 3 * high), :] + total
        sum_ref[rest, :] = base_ref[rest, :]
    else:
        sum_ref[pl.ds(0, 3 * high), :] = total
        sum_ref[rest, 0:LANES] = source[pl.ds(32, 8), :]
        sum_ref[rest, LANES:WIDE] = jnp.zeros((8, WIDE - LANES), jnp.float32)


def spread(column, source, base, groups, columns):
    high = groups * (ND_DEV // WIDE)
    vmem = pl.BlockSpec(memory_space=pltpu.VMEM)
    bases = () if base is None else (base,)
    return pl.pallas_call(
        functools.partial(spread_kernel, groups, columns, base is not None),
        out_shape=jax.ShapeDtypeStruct((3 * high + 8, WIDE), jnp.float32),
        in_specs=[pl.BlockSpec(memory_space=pltpu.SMEM)] + [vmem] * (1 + len(bases)),
        out_specs=vmem,
        scratch_shapes=[
            pltpu.VMEM((6 * high, 8 * LANES), jnp.bfloat16),
            pltpu.VMEM((WIDE, 8 * LANES), jnp.bfloat16),
        ],
        cost_estimate=pl.CostEstimate(
            flops=12 * high * 8 * LANES * WIDE, bytes_accessed=2000000, transcendentals=0
        ),
        compiler_params=pltpu.CompilerParams(vmem_limit_bytes=16 * 1024 * 1024),
    )(column, source, *bases)


def total_kernel(groups, group_ref, *refs):
    partials = refs[:groups]
    grad_ref, part_ref, sum_ref = refs[groups:]
    per_owner = ND_DEV // WIDE
    high = groups * per_owner
    total = partials[0][...]
    for partial in partials[1:]:
        total = total + partial[...]
    sum_ref[...] = total
    design = total[: 3 * high]
    squares = jnp.sum(design * design)
    spent = jnp.sum(total[3 * high : 3 * high + 1])
    lane = lax.broadcasted_iota(jnp.int32, (1, LANES), 1)
    stats = jnp.where(lane == 0, squares, jnp.where(lane == 1, spent, 0.0))
    part_ref[...] = jnp.broadcast_to(stats[None], part_ref.shape)
    for c in range(3):
        start = pl.multiple_of(c * high + group_ref[0] * per_owner, per_owner)
        block = sum_ref[pl.ds(start, per_owner), :]
        for i in range(per_owner):
            grad_ref[c : c + 1, i * WIDE : (i + 1) * WIDE] = block[i : i + 1, :]


def totalled(group, partials, columns):
    groups = len(partials)
    vmem = pl.BlockSpec(memory_space=pltpu.VMEM)
    return pl.pallas_call(
        functools.partial(total_kernel, groups),
        out_shape=(
            jax.ShapeDtypeStruct((3, ND_DEV), jnp.float32),
            jax.ShapeDtypeStruct((columns, 1, LANES), jnp.float32),
        ),
        in_specs=[pl.BlockSpec(memory_space=pltpu.SMEM)] + [vmem] * groups,
        out_specs=(vmem, vmem),
        scratch_shapes=[pltpu.VMEM(partials[0].shape, jnp.float32)],
        compiler_params=pltpu.CompilerParams(vmem_limit_bytes=4 * 1024 * 1024),
    )(group, *partials)


def scale_kernel(over_nodes, over_elements, grad_ref, part_ref, out_ref, objective_ref):
    total = jnp.sum(part_ref[:, 0, :], axis=0, keepdims=True)
    lane = lax.broadcasted_iota(jnp.int32, (1, LANES), 1)
    squares = jnp.sum(jnp.where(lane == 0, total, 0.0), axis=1, keepdims=True)
    spent = jnp.sum(jnp.where(lane == 1, total, 0.0), axis=1, keepdims=True)
    out_ref[...] = grad_ref[...] * lax.rsqrt(squares * over_nodes + 1e-06)
    objective_ref[...] = spent * over_elements


def scaled(grad, parts, over_nodes, over_elements):
    vmem = pl.BlockSpec(memory_space=pltpu.VMEM)
    return pl.pallas_call(
        functools.partial(scale_kernel, over_nodes, over_elements),
        out_shape=(
            jax.ShapeDtypeStruct((3, ND_DEV), jnp.float32),
            jax.ShapeDtypeStruct((1, 1), jnp.float32),
        ),
        in_specs=[vmem, vmem],
        out_specs=(vmem, vmem),
        compiler_params=pltpu.CompilerParams(vmem_limit_bytes=2 * 1024 * 1024),
    )(grad, parts)


def body(velocity, adjoint, spacing, elem_count, design_map):
    slots = velocity.shape[-1]
    groups = lax.axis_size("grp")
    columns = lax.axis_size(ELEM)
    group = lax.axis_index("grp").astype(jnp.int32).reshape(1)
    column = lax.axis_index(ELEM).astype(jnp.int32).reshape(1)
    sent = element_terms(elem_count, velocity, adjoint, spacing, design_map)
    partner = [(e + 1) % columns if e % 2 else (e - 1) % columns for e in range(columns)]
    across = lax.ppermute(sent, ELEM, list(enumerate(partner)))
    within = lax.ppermute(sent, "elem_2", [(0, 1), (1, 0)])
    partial = spread(column, sent, None, groups, columns)
    partial = spread(column, within, partial, groups, columns)
    partial = spread(column, across, partial, groups, columns)
    partials = [partial] + [
        lax.ppermute(partial, "grp", [(i, i ^ by) for i in range(groups)]) for by in (1, 3, 2)
    ]
    grad, parts = totalled(group, partials, columns)
    parts = lax.all_to_all(parts, ELEM, split_axis=0, concat_axis=0, tiled=True)
    devices = groups * columns
    direction, objective = scaled(
        grad,
        parts,
        1.0 / (3.0 * ND_DEV * devices),
        1.0 / (NODES * slots * devices),
    )
    return (direction, objective.reshape(()))


def solution(mesh):
    finer = Mesh(
        mesh.devices.reshape(mesh.shape["grp"], 4, 4, 2), ("grp", "elem_0", "elem_1", "elem_2")
    )
    in_specs = (
        P(None, None, GRP_ELEM),
        P(None, None, GRP_ELEM),
        P(None, GRP_ELEM),
        P(GRP_ELEM),
        P(None, GRP_ELEM),
    )
    out_specs = (P(None, GRP_ELEM), P())
    return jax.shard_map(body, mesh=finer, in_specs=in_specs, out_specs=out_specs, check_vma=False)
```

```python
import functools

import jax
import jax.numpy as jnp
import numpy as np
from jax import lax
from jax.experimental import pallas as pl
from jax.experimental.pallas import tpu as pltpu
from jax.sharding import Mesh
from jax.sharding import PartitionSpec as P

P_SIZE = 7
NODES = P_SIZE**3
ND_DEV = 2048
LANES = 128
ELEM = ("elem_0", "elem_1", "elem_2")
GRP_ELEM = ("grp", "elem_0", "elem_1", "elem_2")
SENT = 40
WIDE = 256
UNROLL = 1
PITCH = 9


def log2(number):
    assert number & (number - 1) == 0
    return number.bit_length() - 1


def lobatto(degree):
    points = np.cos(np.pi * np.arange(degree + 1) / degree)
    for sweep in range(60):
        lower = np.ones(degree + 1)
        upper = points.copy()
        for order in range(2, degree + 1):
            lower, upper = (upper, ((2 * order - 1) * points * upper - (order - 1) * lower) / order)
        points = points - (points * upper - lower) / ((degree + 1) * upper)
    lower = np.ones(degree + 1)
    upper = points.copy()
    for order in range(2, degree + 1):
        lower, upper = (upper, ((2 * order - 1) * points * upper - (order - 1) * lower) / order)
    return (points[::-1].copy(), upper[::-1].copy())


def one_dimensional():
    degree = P_SIZE - 1
    points, values = lobatto(degree)
    weights = 2.0 / (degree * (degree + 1) * values**2)
    derivative = np.zeros((P_SIZE, P_SIZE))
    for i in range(P_SIZE):
        for j in range(P_SIZE):
            if i != j:
                derivative[i, j] = values[i] / (values[j] * (points[i] - points[j]))
    derivative[0, 0] = -degree * (degree + 1) / 4.0
    derivative[degree, degree] = degree * (degree + 1) / 4.0
    points[degree // 2] = 0.0
    derivative[degree // 2, degree // 2] = 0.0
    return (points, weights, derivative)


POINTS, WEIGHTS, DERIVATIVE = one_dimensional()
COLUMN, ACROSS, ALONG, SIGNS = 0, 56, 72, 88
TABLE_ROWS = 144


def table():
    rows = np.zeros((TABLE_ROWS, LANES), np.float32)
    for c in range(P_SIZE):
        rows[COLUMN + 8 * c : COLUMN + 8 * c + P_SIZE] = DERIVATIVE[:, c][:, None]
    rows[ACROSS : ACROSS + P_SIZE] = WEIGHTS[:, None]
    rows[ACROSS + 8 : ACROSS + 8 + P_SIZE] = (WEIGHTS * POINTS)[:, None]
    rows[ALONG : ALONG + P_SIZE] = WEIGHTS[:, None]
    rows[ALONG + 8 : ALONG + 8 + P_SIZE] = (WEIGHTS * POINTS)[:, None]
    for number, axes in enumerate(((0,), (1,), (2,), (0, 1), (0, 2), (1, 2), (0, 1, 2))):
        for vertex in range(8):
            sign = np.prod([2.0 * (vertex >> 2 - m & 1) - 1.0 for m in axes])
            rows[SIGNS + 8 * number + vertex] = sign / 8.0
    return rows


def along_vectors(f):
    half = P_SIZE // 2
    last = P_SIZE - 1
    even = [f[j] + f[last - j] for j in range(half)]
    odd = [f[j] - f[last - j] for j in range(half)]
    out = [None] * P_SIZE
    for i in range(half + 1):
        coef = DERIVATIVE[i]
        b = None
        for j in range(half):
            piece = float((coef[j] - coef[last - j]) / 2) * odd[j]
            b = piece if b is None else b + piece
        if i == half:
            out[i] = b
            continue
        a = float(coef[half]) * f[half]
        for j in range(half):
            a = a + float((coef[j] + coef[last - j]) / 2) * even[j]
        out[i] = b + a
        out[last - i] = b - a
    return out


def terms_kernel(
    count_ref,
    u_hbm,
    w_hbm,
    h_hbm,
    map_hbm,
    tab_hbm,
    out_ref,
    u_ref,
    w_ref,
    h_ref,
    map_ref,
    tab_ref,
    ga_ref,
    gb_ref,
    gc_ref,
    mom_ref,
    sems,
):
    n = P_SIZE
    fields = [(ref, i) for ref in (u_ref, w_ref) for i in range(3)]
    rows = pl.ds(0, n)
    pairs = [(source.at[i], ref.at[i]) for source, ref in ((u_hbm, u_ref), (w_hbm, w_ref)) for i in range(3)]
    pairs += [(tab_hbm, tab_ref), (h_hbm, h_ref), (map_hbm, map_ref)]
    copies = [
        pltpu.make_async_copy(source, target, sems.at[i])
        for i, (source, target) in enumerate(pairs)
    ]
    for copy in copies:
        copy.start()

    def first(f, ref, i, b):
        slabs = [ref[i, pl.ds(a * n * n + b * n, n), :] for a in range(n)]
        for a, value in enumerate(along_vectors(slabs)):
            ga_ref[f, a, b, rows, :] = value

    mom_ref[...] = jnp.zeros_like(mom_ref)
    for f, (ref, i) in enumerate(fields):
        copies[f].wait()

        def step(b, carry, f=f, ref=ref, i=i):
            first(f, ref, i, b)
            return carry

        lax.fori_loop(0, n, step, 0, unroll=UNROLL)
    for copy in copies[6:]:
        copy.wait()

    h = h_ref[...]
    factor = [2.0 / h[j : j + 1] for j in range(3)]
    square = [f * f for f in factor]

    def second(a, carry):
        base = a * n * n
        for f, (ref, i) in enumerate(fields):
            slabs = [ref[i, pl.ds(base + b * n, n), :] for b in range(n)]
            for b, value in enumerate(along_vectors(slabs)):
                gb_ref[f, b, rows, :] = value
            slabs = [ref[i, pl.ds(base + c, n, stride=n), :] for c in range(n)]
            for c, value in enumerate(along_vectors(slabs)):
                gc_ref[pl.ds((f * n + c) * PITCH, n), :] = value
        sums = [[None, None] for _ in range(6)]
        spent = None
        for b in range(n):
            grads = []
            for f in range(6):
                gc = gc_ref[pl.ds(f * n * PITCH + b, n, stride=PITCH), :]
                grads.append([ga_ref[f, a, b, rows, :], gb_ref[f, b, rows, :], gc])
            gu, gw = grads[:3], grads[3:]

            def cross(c, j):
                return gu[0][c] * gw[0][j] + gu[1][c] * gw[1][j] + gu[2][c] * gw[2][j]

            pairs = [cross(0, 0), cross(1, 1), cross(2, 2)]
            pairs += [cross(c, j) + cross(j, c) for c, j in ((0, 1), (0, 2), (1, 2))]
            own = [gu[0][j] * gu[0][j] + gu[1][j] * gu[1][j] + gu[2][j] * gu[2][j] for j in range(3)]
            squared = own[0] * square[0] + own[1] * square[1] + own[2] * square[2]
            weight = float(WEIGHTS[b])
            slope = float(WEIGHTS[b] * POINTS[b])
            for s, value in enumerate(pairs):
                piece = weight * value
                sums[s][0] = piece if sums[s][0] is None else sums[s][0] + piece
                if b != n // 2:
                    piece = slope * value
                    sums[s][1] = piece if sums[s][1] is None else sums[s][1] + piece
            piece = weight * squared
            spent = piece if spent is None else spent + piece
        wa = tab_ref[pl.ds(ALONG + a, 1), :]
        wxa = tab_ref[pl.ds(ALONG + 8 + a, 1), :]
        for s in range(6):
            for r, scale in enumerate((wa, wxa)):
                for t in range(2):
                    at = s * 4 + r * 2 + t
                    mom_ref[at, rows, :] = mom_ref[at, rows, :] + scale * sums[s][t]
        mom_ref[24, rows, :] = mom_ref[24, rows, :] + wa * spent
        return carry

    lax.fori_loop(0, n, second, 0)

    jacobian = h[0:1] * h[1:2] * h[2:3] * 0.125
    lanes = lax.broadcasted_iota(jnp.int32, (1, LANES), 1)
    live = jacobian * (lanes < count_ref[0]).astype(jnp.float32)
    flat = tab_ref[pl.ds(ACROSS, n), :]
    slant = tab_ref[pl.ds(ACROSS + 8, n), :]
    signs = [tab_ref[pl.ds(SIGNS + 8 * i, 8), :] for i in range(7)]

    def moment(value, c):
        return jnp.sum(value * (slant if c else flat), axis=0, keepdims=True)

    def along(axis, part):
        others = [m for m in range(3) if m != axis]
        total = None
        for low in range(2):
            for high in range(2):
                powers = [0, 0, 0]
                powers[others[0]] = low
                powers[others[1]] = high
                axes = tuple(sorted([axis] + [m for m in others if powers[m]]))
                number = {(0,): 0, (1,): 1, (2,): 2, (0, 1): 3, (0, 2): 4, (1, 2): 5, (0, 1, 2): 6}[axes]
                piece = signs[number] * moment(part[powers[0] * 2 + powers[1]], powers[2])
                total = piece if total is None else total + piece
        return total

    mom = [[mom_ref[s * 4 + i, rows, :] for i in range(4)] for s in range(6)]
    inner = [
        square[0] * mom[0][i] + square[1] * mom[1][i] + square[2] * mom[2][i] for i in range(4)
    ]
    between = {(0, 1): 3, (0, 2): 4, (1, 2): 5}
    for c in range(3):
        part = [inner[i] - (2.0 * square[c]) * mom[c][i] for i in range(4)]
        total = along(c, part)
        for j in range(3):
            if j != c:
                shared = mom[between[(min(c, j), max(c, j))]]
                total = total - square[j] * along(j, shared)
        out_ref[pl.ds(8 * c, 8), :] = total * (factor[c] * live)
    out_ref[pl.ds(24, 8), :] = map_ref[...].astype(jnp.float32)
    spent = live * moment(mom_ref[24, rows, :], 0)
    out_ref[pl.ds(32, 8), :] = jnp.broadcast_to(spent, (8, LANES))


def element_terms(count, velocity, adjoint, spacing, design_map):
    vmem = pl.BlockSpec(memory_space=pltpu.VMEM)
    arrays = (velocity, adjoint, spacing, design_map, jnp.asarray(table()))
    arrays = [pltpu.with_memory_space_constraint(array, pltpu.HBM) for array in arrays]
    return pl.pallas_call(
        terms_kernel,
        out_shape=pltpu.VMEM((SENT, LANES), jnp.float32),
        in_specs=[pl.BlockSpec(memory_space=pltpu.SMEM)]
        + [pl.BlockSpec(memory_space=pltpu.HBM)] * 5,
        out_specs=vmem,
        scratch_shapes=[
            pltpu.VMEM(velocity.shape, jnp.float32),
            pltpu.VMEM(adjoint.shape, jnp.float32),
            pltpu.VMEM(spacing.shape, jnp.float32),
            pltpu.VMEM(design_map.shape, jnp.int32),
            pltpu.VMEM((TABLE_ROWS, LANES), jnp.float32),
            pltpu.VMEM((6, P_SIZE, P_SIZE, 8, LANES), jnp.float32),
            pltpu.VMEM((6, P_SIZE, 8, LANES), jnp.float32),
            pltpu.VMEM((6 * P_SIZE * PITCH, LANES), jnp.float32),
            pltpu.VMEM((25, 8, LANES), jnp.float32),
            pltpu.SemaphoreType.DMA((9,)),
        ],
        compiler_params=pltpu.CompilerParams(vmem_limit_bytes=16 * 1024 * 1024),
    )(count, *arrays)


def spread_kernel(groups, columns, adds, column_ref, source, *refs):
    base_ref = refs[0] if adds else None
    sum_ref, left_ref, right_ref = refs[-3:]
    column = column_ref[0]
    per_owner = ND_DEV // WIDE
    high = groups * per_owner
    half = jnp.bfloat16
    tile = (16, LANES)

    def rows_from(count):
        ramp = lax.broadcasted_iota(jnp.int32, (count, LANES), 0).astype(jnp.float32)
        return ramp.astype(half).reshape(count // 16, *tile)

    def spread_row(rows, k):
        return jnp.broadcast_to(rows[k : k + 1], tile).astype(half)[None]

    ramp_wide = rows_from(WIDE)
    ramp_high = rows_from(high)
    node = source[pl.ds(24, 8), :].astype(jnp.int32)
    owner = node >> log2(ND_DEV)
    at = (owner >> log2(columns)) * per_owner + ((node & (ND_DEV - 1)) >> log2(WIDE))
    at = jnp.where((owner & (columns - 1)) == column, at, -1).astype(jnp.float32)
    low = (node & (WIDE - 1)).astype(jnp.float32)
    parts = []
    for c in range(3):
        value = source[pl.ds(8 * c, 8), :]
        coarse = value.astype(half).astype(jnp.float32)
        parts.append((coarse, value - coarse))
    one = jnp.ones((), half)
    zero = jnp.zeros((), half)
    for k in range(8):
        lanes = pl.ds(k * LANES, LANES)
        mask = jnp.where(ramp_wide == spread_row(low, k), one, zero)
        right_ref[:, lanes] = mask.reshape(WIDE, LANES)
        hit = ramp_high == spread_row(at, k)
        for c in range(3):
            for piece in range(2):
                placed = jnp.where(hit, spread_row(parts[c][piece], k), zero)
                left_ref[pl.ds((piece * 3 + c) * high, high), lanes] = placed.reshape(high, LANES)
    both = lax.dot_general(
        left_ref[...],
        right_ref[...],
        (((1,), (1,)), ((), ())),
        preferred_element_type=jnp.float32,
    )
    total = both[: 3 * high] + both[3 * high :]
    rest = pl.ds(3 * high, 8)
    if adds:
        sum_ref[pl.ds(0, 3 * high), :] = base_ref[pl.ds(0, 3 * high), :] + total
        sum_ref[rest, :] = base_ref[rest, :]
    else:
        sum_ref[pl.ds(0, 3 * high), :] = total
        sum_ref[rest, 0:LANES] = source[pl.ds(32, 8), :]
        sum_ref[rest, LANES:WIDE] = jnp.zeros((8, WIDE - LANES), jnp.float32)


def spread(column, source, base, groups, columns):
    high = groups * (ND_DEV // WIDE)
    vmem = pl.BlockSpec(memory_space=pltpu.VMEM)
    bases = () if base is None else (base,)
    return pl.pallas_call(
        functools.partial(spread_kernel, groups, columns, base is not None),
        out_shape=jax.ShapeDtypeStruct((3 * high + 8, WIDE), jnp.float32),
        in_specs=[pl.BlockSpec(memory_space=pltpu.SMEM)] + [vmem] * (1 + len(bases)),
        out_specs=vmem,
        scratch_shapes=[
            pltpu.VMEM((6 * high, 8 * LANES), jnp.bfloat16),
            pltpu.VMEM((WIDE, 8 * LANES), jnp.bfloat16),
        ],
        cost_estimate=pl.CostEstimate(
            flops=12 * high * 8 * LANES * WIDE, bytes_accessed=2000000, transcendentals=0
        ),
        compiler_params=pltpu.CompilerParams(vmem_limit_bytes=16 * 1024 * 1024),
    )(column, source, *bases)


def total_kernel(groups, group_ref, *refs):
    partials = refs[:groups]
    grad_ref, part_ref, sum_ref = refs[groups:]
    per_owner = ND_DEV // WIDE
    high = groups * per_owner
    total = partials[0][...]
    for partial in partials[1:]:
        total = total + partial[...]
    sum_ref[...] = total
    design = total[: 3 * high]
    squares = jnp.sum(design * design)
    spent = jnp.sum(total[3 * high : 3 * high + 1])
    lane = lax.broadcasted_iota(jnp.int32, (1, LANES), 1)
    stats = jnp.where(lane == 0, squares, jnp.where(lane == 1, spent, 0.0))
    part_ref[...] = jnp.broadcast_to(stats[None], part_ref.shape)
    for c in range(3):
        start = pl.multiple_of(c * high + group_ref[0] * per_owner, per_owner)
        block = sum_ref[pl.ds(start, per_owner), :]
        for i in range(per_owner):
            grad_ref[c : c + 1, i * WIDE : (i + 1) * WIDE] = block[i : i + 1, :]


def totalled(group, partials, columns):
    groups = len(partials)
    vmem = pl.BlockSpec(memory_space=pltpu.VMEM)
    return pl.pallas_call(
        functools.partial(total_kernel, groups),
        out_shape=(
            jax.ShapeDtypeStruct((3, ND_DEV), jnp.float32),
            jax.ShapeDtypeStruct((columns, 1, LANES), jnp.float32),
        ),
        in_specs=[pl.BlockSpec(memory_space=pltpu.SMEM)] + [vmem] * groups,
        out_specs=(vmem, vmem),
        scratch_shapes=[pltpu.VMEM(partials[0].shape, jnp.float32)],
        compiler_params=pltpu.CompilerParams(vmem_limit_bytes=4 * 1024 * 1024),
    )(group, *partials)


def scale_kernel(over_nodes, over_elements, grad_ref, part_ref, out_ref, objective_ref):
    total = jnp.sum(part_ref[:, 0, :], axis=0, keepdims=True)
    lane = lax.broadcasted_iota(jnp.int32, (1, LANES), 1)
    squares = jnp.sum(jnp.where(lane == 0, total, 0.0), axis=1, keepdims=True)
    spent = jnp.sum(jnp.where(lane == 1, total, 0.0), axis=1, keepdims=True)
    out_ref[...] = grad_ref[...] * lax.rsqrt(squares * over_nodes + 1e-06)
    objective_ref[...] = spent * over_elements


def scaled(grad, parts, over_nodes, over_elements):
    vmem = pl.BlockSpec(memory_space=pltpu.VMEM)
    return pl.pallas_call(
        functools.partial(scale_kernel, over_nodes, over_elements),
        out_shape=(
            jax.ShapeDtypeStruct((3, ND_DEV), jnp.float32),
            jax.ShapeDtypeStruct((1, 1), jnp.float32),
        ),
        in_specs=[vmem, vmem],
        out_specs=(vmem, vmem),
        compiler_params=pltpu.CompilerParams(vmem_limit_bytes=2 * 1024 * 1024),
    )(grad, parts)


def body(velocity, adjoint, spacing, elem_count, design_map):
    slots = velocity.shape[-1]
    groups = lax.axis_size("grp")
    columns = lax.axis_size(ELEM)
    group = lax.axis_index("grp").astype(jnp.int32).reshape(1)
    column = lax.axis_index(ELEM).astype(jnp.int32).reshape(1)
    sent = element_terms(elem_count, velocity, adjoint, spacing, design_map)
    partner = [(e + 1) % columns if e % 2 else (e - 1) % columns for e in range(columns)]
    within = lax.ppermute(sent, "elem_2", [(0, 1), (1, 0)])
    across = lax.ppermute(sent, ELEM, list(enumerate(partner)))
    partial = spread(column, sent, None, groups, columns)
    partial = spread(column, within, partial, groups, columns)
    partial = spread(column, across, partial, groups, columns)
    partials = [partial] + [
        lax.ppermute(partial, "grp", [(i, i ^ by) for i in range(groups)]) for by in (1, 3, 2)
    ]
    grad, parts = totalled(group, partials, columns)
    parts = lax.all_to_all(parts, ELEM, split_axis=0, concat_axis=0, tiled=True)
    devices = groups * columns
    direction, objective = scaled(
        grad,
        parts,
        1.0 / (3.0 * ND_DEV * devices),
        1.0 / (NODES * slots * devices),
    )
    return (direction, objective.reshape(()))


def solution(mesh):
    finer = Mesh(
        mesh.devices.reshape(mesh.shape["grp"], 4, 4, 2), ("grp", "elem_0", "elem_1", "elem_2")
    )
    in_specs = (
        P(None, None, GRP_ELEM),
        P(None, None, GRP_ELEM),
        P(None, GRP_ELEM),
        P(GRP_ELEM),
        P(None, GRP_ELEM),
    )
    out_specs = (P(None, GRP_ELEM), P())
    return jax.shard_map(body, mesh=finer, in_specs=in_specs, out_specs=out_specs, check_vma=False)
```

```python
import functools

import jax
import jax.numpy as jnp
import numpy as np
from jax import lax
from jax.experimental import pallas as pl
from jax.experimental.pallas import tpu as pltpu
from jax.sharding import Mesh
from jax.sharding import PartitionSpec as P

P_SIZE = 7
NODES = P_SIZE**3
ND_DEV = 2048
LANES = 128
ELEM = ("elem_0", "elem_1", "elem_2")
GRP_ELEM = ("grp", "elem_0", "elem_1", "elem_2")
SENT = 40
WIDE = 128
UNROLL = 1
PITCH = 9


def log2(number):
    assert number & (number - 1) == 0
    return number.bit_length() - 1


def lobatto(degree):
    points = np.cos(np.pi * np.arange(degree + 1) / degree)
    for sweep in range(60):
        lower = np.ones(degree + 1)
        upper = points.copy()
        for order in range(2, degree + 1):
            lower, upper = (upper, ((2 * order - 1) * points * upper - (order - 1) * lower) / order)
        points = points - (points * upper - lower) / ((degree + 1) * upper)
    lower = np.ones(degree + 1)
    upper = points.copy()
    for order in range(2, degree + 1):
        lower, upper = (upper, ((2 * order - 1) * points * upper - (order - 1) * lower) / order)
    return (points[::-1].copy(), upper[::-1].copy())


def one_dimensional():
    degree = P_SIZE - 1
    points, values = lobatto(degree)
    weights = 2.0 / (degree * (degree + 1) * values**2)
    derivative = np.zeros((P_SIZE, P_SIZE))
    for i in range(P_SIZE):
        for j in range(P_SIZE):
            if i != j:
                derivative[i, j] = values[i] / (values[j] * (points[i] - points[j]))
    derivative[0, 0] = -degree * (degree + 1) / 4.0
    derivative[degree, degree] = degree * (degree + 1) / 4.0
    points[degree // 2] = 0.0
    derivative[degree // 2, degree // 2] = 0.0
    return (points, weights, derivative)


POINTS, WEIGHTS, DERIVATIVE = one_dimensional()
ACROSS, ALONG, SIGNS = 0, 16, 32
TABLE_ROWS = 88


def table():
    rows = np.zeros((TABLE_ROWS, LANES), np.float32)
    rows[ACROSS : ACROSS + P_SIZE] = WEIGHTS[:, None]
    rows[ACROSS + 8 : ACROSS + 8 + P_SIZE] = (WEIGHTS * POINTS)[:, None]
    rows[ALONG : ALONG + P_SIZE] = WEIGHTS[:, None]
    rows[ALONG + 8 : ALONG + 8 + P_SIZE] = (WEIGHTS * POINTS)[:, None]
    for number, axes in enumerate(((0,), (1,), (2,), (0, 1), (0, 2), (1, 2), (0, 1, 2))):
        for vertex in range(8):
            sign = np.prod([2.0 * (vertex >> 2 - m & 1) - 1.0 for m in axes])
            rows[SIGNS + 8 * number + vertex] = sign / 8.0
    return rows


def along_vectors(f):
    half = P_SIZE // 2
    last = P_SIZE - 1
    even = [f[j] + f[last - j] for j in range(half)]
    odd = [f[j] - f[last - j] for j in range(half)]
    out = [None] * P_SIZE
    for i in range(half + 1):
        coef = DERIVATIVE[i]
        b = None
        for j in range(half):
            piece = float((coef[j] - coef[last - j]) / 2) * odd[j]
            b = piece if b is None else b + piece
        if i == half:
            out[i] = b
            continue
        a = float(coef[half]) * f[half]
        for j in range(half):
            a = a + float((coef[j] + coef[last - j]) / 2) * even[j]
        out[i] = b + a
        out[last - i] = b - a
    return out


def terms_kernel(
    count_ref,
    u_hbm,
    w_hbm,
    h_hbm,
    map_hbm,
    tab_hbm,
    out_ref,
    u_ref,
    w_ref,
    h_ref,
    map_ref,
    tab_ref,
    ga_ref,
    gb_ref,
    gc_ref,
    mom_ref,
    sems,
):
    n = P_SIZE
    fields = [(ref, i) for ref in (u_ref, w_ref) for i in range(3)]
    rows = pl.ds(0, n)
    pairs = [(source.at[i], ref.at[i]) for source, ref in ((u_hbm, u_ref), (w_hbm, w_ref)) for i in range(3)]
    pairs += [(tab_hbm, tab_ref), (h_hbm, h_ref), (map_hbm, map_ref)]
    copies = [
        pltpu.make_async_copy(source, target, sems.at[i])
        for i, (source, target) in enumerate(pairs)
    ]
    for copy in copies:
        copy.start()

    def first(f, ref, i, b):
        slabs = [ref[i, pl.ds(a * n * n + b * n, n), :] for a in range(n)]
        for a, value in enumerate(along_vectors(slabs)):
            ga_ref[f, a, b, rows, :] = value

    mom_ref[...] = jnp.zeros_like(mom_ref)
    for f, (ref, i) in enumerate(fields):
        copies[f].wait()

        def step(b, carry, f=f, ref=ref, i=i):
            first(f, ref, i, b)
            return carry

        lax.fori_loop(0, n, step, 0, unroll=UNROLL)
    for copy in copies[6:]:
        copy.wait()

    h = h_ref[...]
    factor = [2.0 / h[j : j + 1] for j in range(3)]
    square = [f * f for f in factor]

    def second(a, carry):
        base = a * n * n
        for f, (ref, i) in enumerate(fields):
            slabs = [ref[i, pl.ds(base + b * n, n), :] for b in range(n)]
            for b, value in enumerate(along_vectors(slabs)):
                gb_ref[f, b, rows, :] = value
            slabs = [ref[i, pl.ds(base + c, n, stride=n), :] for c in range(n)]
            for c, value in enumerate(along_vectors(slabs)):
                gc_ref[pl.ds((f * n + c) * PITCH, n), :] = value
        sums = [[None, None] for _ in range(6)]
        kept = [None] * 6
        spent = None
        for b in [0, 6, 1, 5, 2, 4, 3]:
            grads = []
            for f in range(6):
                gc = gc_ref[pl.ds(f * n * PITCH + b, n, stride=PITCH), :]
                grads.append([ga_ref[f, a, b, rows, :], gb_ref[f, b, rows, :], gc])
            gu, gw = grads[:3], grads[3:]

            def cross(c, j):
                return gu[0][c] * gw[0][j] + gu[1][c] * gw[1][j] + gu[2][c] * gw[2][j]

            pairs = [cross(0, 0), cross(1, 1), cross(2, 2)]
            pairs += [cross(c, j) + cross(j, c) for c, j in ((0, 1), (0, 2), (1, 2))]
            own = [gu[0][j] * gu[0][j] + gu[1][j] * gu[1][j] + gu[2][j] * gu[2][j] for j in range(3)]
            squared = own[0] * square[0] + own[1] * square[1] + own[2] * square[2]
            for s, value in enumerate(pairs):
                if b < n // 2:
                    kept[s] = value
                    continue
                if b == n // 2:
                    sums[s][0] = sums[s][0] + float(WEIGHTS[b]) * value
                    continue
                total = float(WEIGHTS[b]) * (value + kept[s])
                slope = float(WEIGHTS[b] * POINTS[b]) * (value - kept[s])
                sums[s][0] = total if sums[s][0] is None else sums[s][0] + total
                sums[s][1] = slope if sums[s][1] is None else sums[s][1] + slope
            piece = float(WEIGHTS[b]) * squared
            spent = piece if spent is None else spent + piece
        wa = tab_ref[pl.ds(ALONG + a, 1), :]
        wxa = tab_ref[pl.ds(ALONG + 8 + a, 1), :]
        for s in range(6):
            for r, scale in enumerate((wa, wxa)):
                for t in range(2):
                    at = s * 4 + r * 2 + t
                    mom_ref[at, rows, :] = mom_ref[at, rows, :] + scale * sums[s][t]
        mom_ref[24, rows, :] = mom_ref[24, rows, :] + wa * spent
        return carry

    lax.fori_loop(0, n, second, 0, unroll=n)

    jacobian = h[0:1] * h[1:2] * h[2:3] * 0.125
    lanes = lax.broadcasted_iota(jnp.int32, (1, LANES), 1)
    live = jacobian * (lanes < count_ref[0]).astype(jnp.float32)
    flat = tab_ref[pl.ds(ACROSS, n), :]
    slant = tab_ref[pl.ds(ACROSS + 8, n), :]
    signs = [tab_ref[pl.ds(SIGNS + 8 * i, 8), :] for i in range(7)]

    def moment(value, c):
        return jnp.sum(value * (slant if c else flat), axis=0, keepdims=True)

    def along(axis, part):
        others = [m for m in range(3) if m != axis]
        total = None
        for low in range(2):
            for high in range(2):
                powers = [0, 0, 0]
                powers[others[0]] = low
                powers[others[1]] = high
                axes = tuple(sorted([axis] + [m for m in others if powers[m]]))
                number = {(0,): 0, (1,): 1, (2,): 2, (0, 1): 3, (0, 2): 4, (1, 2): 5, (0, 1, 2): 6}[axes]
                piece = signs[number] * moment(part[powers[0] * 2 + powers[1]], powers[2])
                total = piece if total is None else total + piece
        return total

    mom = [[mom_ref[s * 4 + i, rows, :] for i in range(4)] for s in range(6)]
    inner = [
        square[0] * mom[0][i] + square[1] * mom[1][i] + square[2] * mom[2][i] for i in range(4)
    ]
    between = {(0, 1): 3, (0, 2): 4, (1, 2): 5}
    for c in range(3):
        part = [inner[i] - (2.0 * square[c]) * mom[c][i] for i in range(4)]
        total = along(c, part)
        for j in range(3):
            if j != c:
                shared = mom[between[(min(c, j), max(c, j))]]
                total = total - square[j] * along(j, shared)
        out_ref[pl.ds(8 * c, 8), :] = total * (factor[c] * live)
    out_ref[pl.ds(24, 8), :] = map_ref[...].astype(jnp.float32)
    spent = live * moment(mom_ref[24, rows, :], 0)
    out_ref[pl.ds(32, 8), :] = jnp.broadcast_to(spent, (8, LANES))


def element_terms(count, velocity, adjoint, spacing, design_map):
    vmem = pl.BlockSpec(memory_space=pltpu.VMEM)
    arrays = (velocity, adjoint, spacing, design_map, jnp.asarray(table()))
    arrays = [pltpu.with_memory_space_constraint(array, pltpu.HBM) for array in arrays]
    return pl.pallas_call(
        terms_kernel,
        out_shape=pltpu.VMEM((SENT, LANES), jnp.float32),
        in_specs=[pl.BlockSpec(memory_space=pltpu.SMEM)]
        + [pl.BlockSpec(memory_space=pltpu.HBM)] * 5,
        out_specs=vmem,
        scratch_shapes=[
            pltpu.VMEM(velocity.shape, jnp.float32),
            pltpu.VMEM(adjoint.shape, jnp.float32),
            pltpu.VMEM(spacing.shape, jnp.float32),
            pltpu.VMEM(design_map.shape, jnp.int32),
            pltpu.VMEM((TABLE_ROWS, LANES), jnp.float32),
            pltpu.VMEM((6, P_SIZE, P_SIZE, 8, LANES), jnp.float32),
            pltpu.VMEM((6, P_SIZE, 8, LANES), jnp.float32),
            pltpu.VMEM((6 * P_SIZE * PITCH, LANES), jnp.float32),
            pltpu.VMEM((25, 8, LANES), jnp.float32),
            pltpu.SemaphoreType.DMA((9,)),
        ],
        compiler_params=pltpu.CompilerParams(vmem_limit_bytes=16 * 1024 * 1024),
    )(count, *arrays)


def spread_kernel(groups, columns, count, column_ref, *refs):
    sources = refs[:count]
    adds = len(refs) > count + 3
    base_ref = refs[count]
    sum_ref, left_ref, right_ref = refs[-3:]
    column = column_ref[0]
    per_owner = ND_DEV // WIDE
    high = groups * per_owner
    half = jnp.bfloat16
    tile = (16, LANES)

    def rows_from(count):
        ramp = lax.broadcasted_iota(jnp.int32, (count, LANES), 0).astype(jnp.float32)
        return ramp.astype(half).reshape(count // 16, *tile)

    def spread_row(rows, k):
        return jnp.broadcast_to(rows[k : k + 1], tile).astype(half)[None]

    ramp_wide = rows_from(WIDE)
    ramp_high = rows_from(high)
    one = jnp.ones((), half)
    zero = jnp.zeros((), half)
    for s, source in enumerate(sources):
        node = source[pl.ds(24, 8), :].astype(jnp.int32)
        owner = node >> log2(ND_DEV)
        at = (owner >> log2(columns)) * per_owner + ((node & (ND_DEV - 1)) >> log2(WIDE))
        at = jnp.where((owner & (columns - 1)) == column, at, -1).astype(jnp.float32)
        low = (node & (WIDE - 1)).astype(jnp.float32)
        parts = []
        for c in range(3):
            value = source[pl.ds(8 * c, 8), :]
            coarse = value.astype(half).astype(jnp.float32)
            parts.append((coarse, value - coarse))
        for k in range(8):
            lanes = pl.ds((8 * s + k) * LANES, LANES)
            mask = jnp.where(ramp_wide == spread_row(low, k), one, zero)
            right_ref[:, lanes] = mask.reshape(WIDE, LANES)
            hit = ramp_high == spread_row(at, k)
            for c in range(3):
                for piece in range(2):
                    placed = jnp.where(hit, spread_row(parts[c][piece], k), zero)
                    left_ref[pl.ds((piece * 3 + c) * high, high), lanes] = placed.reshape(high, LANES)
    both = lax.dot_general(
        left_ref[...],
        right_ref[...],
        (((1,), (1,)), ((), ())),
        preferred_element_type=jnp.float32,
    )
    total = both[: 3 * high] + both[3 * high :]
    rest = pl.ds(3 * high, 8)
    if adds:
        sum_ref[pl.ds(0, 3 * high), :] = base_ref[pl.ds(0, 3 * high), :] + total
        sum_ref[rest, :] = base_ref[rest, :]
    else:
        sum_ref[pl.ds(0, 3 * high), :] = total
        sum_ref[rest, 0:LANES] = sources[0][pl.ds(32, 8), :]


def spread(column, sources, base, groups, columns):
    count = len(sources)
    high = groups * (ND_DEV // WIDE)
    vmem = pl.BlockSpec(memory_space=pltpu.VMEM)
    bases = () if base is None else (base,)
    return pl.pallas_call(
        functools.partial(spread_kernel, groups, columns, count),
        out_shape=jax.ShapeDtypeStruct((3 * high + 8, WIDE), jnp.float32),
        in_specs=[pl.BlockSpec(memory_space=pltpu.SMEM)] + [vmem] * (count + len(bases)),
        out_specs=vmem,
        scratch_shapes=[
            pltpu.VMEM((6 * high, count * 8 * LANES), jnp.bfloat16),
            pltpu.VMEM((WIDE, count * 8 * LANES), jnp.bfloat16),
        ],
        cost_estimate=pl.CostEstimate(
            flops=12 * high * count * 8 * LANES * WIDE, bytes_accessed=2000000, transcendentals=0
        ),
        compiler_params=pltpu.CompilerParams(vmem_limit_bytes=16 * 1024 * 1024),
    )(column, *sources, *bases)


def total_kernel(groups, group_ref, *refs):
    partials = refs[:groups]
    grad_ref, part_ref, sum_ref = refs[groups:]
    per_owner = ND_DEV // WIDE
    high = groups * per_owner
    total = partials[0][...]
    for partial in partials[1:]:
        total = total + partial[...]
    sum_ref[...] = total
    design = total[: 3 * high]
    squares = jnp.sum(design * design)
    spent = jnp.sum(total[3 * high : 3 * high + 1])
    lane = lax.broadcasted_iota(jnp.int32, (1, LANES), 1)
    stats = jnp.where(lane == 0, squares, jnp.where(lane == 1, spent, 0.0))
    part_ref[...] = jnp.broadcast_to(stats[None], part_ref.shape)
    for c in range(3):
        start = pl.multiple_of(c * high + group_ref[0] * per_owner, per_owner)
        block = sum_ref[pl.ds(start, per_owner), :]
        for i in range(per_owner):
            grad_ref[c : c + 1, i * WIDE : (i + 1) * WIDE] = block[i : i + 1, :]


def totalled(group, partials, columns):
    groups = len(partials)
    vmem = pl.BlockSpec(memory_space=pltpu.VMEM)
    return pl.pallas_call(
        functools.partial(total_kernel, groups),
        out_shape=(
            jax.ShapeDtypeStruct((3, ND_DEV), jnp.float32),
            jax.ShapeDtypeStruct((columns, 1, LANES), jnp.float32),
        ),
        in_specs=[pl.BlockSpec(memory_space=pltpu.SMEM)] + [vmem] * groups,
        out_specs=(vmem, vmem),
        scratch_shapes=[pltpu.VMEM(partials[0].shape, jnp.float32)],
        compiler_params=pltpu.CompilerParams(vmem_limit_bytes=4 * 1024 * 1024),
    )(group, *partials)


def scale_kernel(over_nodes, over_elements, grad_ref, part_ref, out_ref, objective_ref):
    total = jnp.sum(part_ref[:, 0, :], axis=0, keepdims=True)
    lane = lax.broadcasted_iota(jnp.int32, (1, LANES), 1)
    squares = jnp.sum(jnp.where(lane == 0, total, 0.0), axis=1, keepdims=True)
    spent = jnp.sum(jnp.where(lane == 1, total, 0.0), axis=1, keepdims=True)
    out_ref[...] = grad_ref[...] * lax.rsqrt(squares * over_nodes + 1e-06)
    objective_ref[...] = spent * over_elements


def scaled(grad, parts, over_nodes, over_elements):
    vmem = pl.BlockSpec(memory_space=pltpu.VMEM)
    return pl.pallas_call(
        functools.partial(scale_kernel, over_nodes, over_elements),
        out_shape=(
            jax.ShapeDtypeStruct((3, ND_DEV), jnp.float32),
            jax.ShapeDtypeStruct((1, 1), jnp.float32),
        ),
        in_specs=[vmem, vmem],
        out_specs=(vmem, vmem),
        compiler_params=pltpu.CompilerParams(vmem_limit_bytes=2 * 1024 * 1024),
    )(grad, parts)


def body(velocity, adjoint, spacing, elem_count, design_map):
    slots = velocity.shape[-1]
    groups = lax.axis_size("grp")
    columns = lax.axis_size(ELEM)
    group = lax.axis_index("grp").astype(jnp.int32).reshape(1)
    column = lax.axis_index(ELEM).astype(jnp.int32).reshape(1)
    sent = element_terms(elem_count, velocity, adjoint, spacing, design_map)
    partner = [(e + 1) % columns if e % 2 else (e - 1) % columns for e in range(columns)]
    within = lax.ppermute(sent, "elem_2", [(0, 1), (1, 0)])
    across = lax.ppermute(sent, ELEM, list(enumerate(partner)))
    partial = spread(column, (sent,), None, groups, columns)
    partial = spread(column, (within, across), partial, groups, columns)
    partials = [partial] + [
        lax.ppermute(partial, "grp", [(i, i ^ by) for i in range(groups)]) for by in (1, 3, 2)
    ]
    grad, parts = totalled(group, partials, columns)
    parts = lax.all_to_all(parts, ELEM, split_axis=0, concat_axis=0, tiled=True)
    devices = groups * columns
    direction, objective = scaled(
        grad,
        parts,
        1.0 / (3.0 * ND_DEV * devices),
        1.0 / (NODES * slots * devices),
    )
    return (direction, objective.reshape(()))


def solution(mesh):
    finer = Mesh(
        mesh.devices.reshape(mesh.shape["grp"], 4, 4, 2), ("grp", "elem_0", "elem_1", "elem_2")
    )
    in_specs = (
        P(None, None, GRP_ELEM),
        P(None, None, GRP_ELEM),
        P(None, GRP_ELEM),
        P(GRP_ELEM),
        P(None, GRP_ELEM),
    )
    out_specs = (P(None, GRP_ELEM), P())
    return jax.shard_map(body, mesh=finer, in_specs=in_specs, out_specs=out_specs, check_vma=False)
```

```python
import functools

import jax
import jax.numpy as jnp
import numpy as np
from jax import lax
from jax.experimental import pallas as pl
from jax.experimental.pallas import tpu as pltpu
from jax.sharding import Mesh
from jax.sharding import PartitionSpec as P

P_SIZE = 7
NODES = P_SIZE**3
ND_DEV = 2048
LANES = 128
ELEM = ("elem_0", "elem_1", "elem_2")
GRP_ELEM = ("grp", "elem_0", "elem_1", "elem_2")
SENT = 40
WIDE = 128
UNROLL = 1
PITCH = 9


def log2(number):
    assert number & (number - 1) == 0
    return number.bit_length() - 1


def lobatto(degree):
    points = np.cos(np.pi * np.arange(degree + 1) / degree)
    for sweep in range(60):
        lower = np.ones(degree + 1)
        upper = points.copy()
        for order in range(2, degree + 1):
            lower, upper = (upper, ((2 * order - 1) * points * upper - (order - 1) * lower) / order)
        points = points - (points * upper - lower) / ((degree + 1) * upper)
    lower = np.ones(degree + 1)
    upper = points.copy()
    for order in range(2, degree + 1):
        lower, upper = (upper, ((2 * order - 1) * points * upper - (order - 1) * lower) / order)
    return (points[::-1].copy(), upper[::-1].copy())


def one_dimensional():
    degree = P_SIZE - 1
    points, values = lobatto(degree)
    weights = 2.0 / (degree * (degree + 1) * values**2)
    derivative = np.zeros((P_SIZE, P_SIZE))
    for i in range(P_SIZE):
        for j in range(P_SIZE):
            if i != j:
                derivative[i, j] = values[i] / (values[j] * (points[i] - points[j]))
    derivative[0, 0] = -degree * (degree + 1) / 4.0
    derivative[degree, degree] = degree * (degree + 1) / 4.0
    points[degree // 2] = 0.0
    derivative[degree // 2, degree // 2] = 0.0
    return (points, weights, derivative)


POINTS, WEIGHTS, DERIVATIVE = one_dimensional()
ACROSS, ALONG, SIGNS = 0, 16, 32
TABLE_ROWS = 88


def table():
    rows = np.zeros((TABLE_ROWS, LANES), np.float32)
    rows[ACROSS : ACROSS + P_SIZE] = WEIGHTS[:, None]
    rows[ACROSS + 8 : ACROSS + 8 + P_SIZE] = (WEIGHTS * POINTS)[:, None]
    rows[ALONG : ALONG + P_SIZE] = WEIGHTS[:, None]
    rows[ALONG + 8 : ALONG + 8 + P_SIZE] = (WEIGHTS * POINTS)[:, None]
    for number, axes in enumerate(((0,), (1,), (2,), (0, 1), (0, 2), (1, 2), (0, 1, 2))):
        for vertex in range(8):
            sign = np.prod([2.0 * (vertex >> 2 - m & 1) - 1.0 for m in axes])
            rows[SIGNS + 8 * number + vertex] = sign / 8.0
    return rows


def along_vectors(f):
    half = P_SIZE // 2
    last = P_SIZE - 1
    even = [f[j] + f[last - j] for j in range(half)]
    odd = [f[j] - f[last - j] for j in range(half)]
    out = [None] * P_SIZE
    for i in range(half + 1):
        coef = DERIVATIVE[i]
        b = None
        for j in range(half):
            piece = float((coef[j] - coef[last - j]) / 2) * odd[j]
            b = piece if b is None else b + piece
        if i == half:
            out[i] = b
            continue
        a = float(coef[half]) * f[half]
        for j in range(half):
            a = a + float((coef[j] + coef[last - j]) / 2) * even[j]
        out[i] = b + a
        out[last - i] = b - a
    return out


def terms_kernel(
    count_ref,
    u_hbm,
    w_hbm,
    h_hbm,
    map_hbm,
    tab_hbm,
    out_ref,
    u_ref,
    w_ref,
    h_ref,
    map_ref,
    tab_ref,
    ga_ref,
    gb_ref,
    gc_ref,
    mom_ref,
    sems,
):
    n = P_SIZE
    fields = [(ref, i) for ref in (u_ref, w_ref) for i in range(3)]
    rows = pl.ds(0, n)
    whole = pl.ds(0, NODES)
    pairs = [
        (source.at[i], ref.at[i, whole])
        for source, ref in ((u_hbm, u_ref), (w_hbm, w_ref))
        for i in range(3)
    ]
    pairs += [(tab_hbm, tab_ref), (h_hbm, h_ref), (map_hbm, map_ref)]
    copies = [
        pltpu.make_async_copy(source, target, sems.at[i])
        for i, (source, target) in enumerate(pairs)
    ]
    for copy in copies:
        copy.start()

    def first(f, ref, i, b):
        slabs = [ref[i, pl.ds(a * n * n + b * n, n), :] for a in range(n)]
        for a, value in enumerate(along_vectors(slabs)):
            ga_ref[f, a, b, rows, :] = value

    mom_ref[...] = jnp.zeros_like(mom_ref)
    for f, (ref, i) in enumerate(fields):
        copies[f].wait()

        def step(b, carry, f=f, ref=ref, i=i):
            first(f, ref, i, b)
            return carry

        lax.fori_loop(0, n, step, 0, unroll=UNROLL)
    for copy in copies[6:]:
        copy.wait()

    h = h_ref[...]
    factor = [2.0 / h[j : j + 1] for j in range(3)]
    square = [f * f for f in factor]

    def second(a, carry):
        base = a * n * n
        for f, (ref, i) in enumerate(fields):
            slabs = [ref[i, pl.ds(base + b * n, n), :] for b in range(n)]
            for b, value in enumerate(along_vectors(slabs)):
                gb_ref[f, b, rows, :] = value
            slabs = [ref[i, pl.ds(base + c, n, stride=n), :] for c in range(n)]
            for c, value in enumerate(along_vectors(slabs)):
                gc_ref[pl.ds((f * n + c) * PITCH, n), :] = value
        sums = [[None, None] for _ in range(6)]
        kept = [None] * 6
        spent = None
        for b in [0, 6, 1, 5, 2, 4, 3]:
            grads = []
            for f in range(6):
                gc = gc_ref[pl.ds(f * n * PITCH + b, n, stride=PITCH), :]
                grads.append([ga_ref[f, a, b, rows, :], gb_ref[f, b, rows, :], gc])
            gu, gw = grads[:3], grads[3:]

            def cross(c, j):
                return gu[0][c] * gw[0][j] + gu[1][c] * gw[1][j] + gu[2][c] * gw[2][j]

            pairs = [cross(0, 0), cross(1, 1), cross(2, 2)]
            pairs += [cross(c, j) + cross(j, c) for c, j in ((0, 1), (0, 2), (1, 2))]
            own = [gu[0][j] * gu[0][j] + gu[1][j] * gu[1][j] + gu[2][j] * gu[2][j] for j in range(3)]
            squared = own[0] * square[0] + own[1] * square[1] + own[2] * square[2]
            for s, value in enumerate(pairs):
                if b < n // 2:
                    kept[s] = value
                    continue
                if b == n // 2:
                    sums[s][0] = sums[s][0] + float(WEIGHTS[b]) * value
                    continue
                total = float(WEIGHTS[b]) * (value + kept[s])
                slope = float(WEIGHTS[b] * POINTS[b]) * (value - kept[s])
                sums[s][0] = total if sums[s][0] is None else sums[s][0] + total
                sums[s][1] = slope if sums[s][1] is None else sums[s][1] + slope
            piece = float(WEIGHTS[b]) * squared
            spent = piece if spent is None else spent + piece
        wa = tab_ref[pl.ds(ALONG + a, 1), :]
        wxa = tab_ref[pl.ds(ALONG + 8 + a, 1), :]
        for s in range(6):
            for r, scale in enumerate((wa, wxa)):
                for t in range(2):
                    at = s * 4 + r * 2 + t
                    mom_ref[at, rows, :] = mom_ref[at, rows, :] + scale * sums[s][t]
        mom_ref[24, rows, :] = mom_ref[24, rows, :] + wa * spent
        return carry

    lax.fori_loop(0, n, second, 0, unroll=n)

    jacobian = h[0:1] * h[1:2] * h[2:3] * 0.125
    lanes = lax.broadcasted_iota(jnp.int32, (1, LANES), 1)
    live = jacobian * (lanes < count_ref[0]).astype(jnp.float32)
    flat = tab_ref[pl.ds(ACROSS, n), :]
    slant = tab_ref[pl.ds(ACROSS + 8, n), :]
    signs = [tab_ref[pl.ds(SIGNS + 8 * i, 8), :] for i in range(7)]

    def moment(value, c):
        return jnp.sum(value * (slant if c else flat), axis=0, keepdims=True)

    def along(axis, part):
        others = [m for m in range(3) if m != axis]
        total = None
        for low in range(2):
            for high in range(2):
                powers = [0, 0, 0]
                powers[others[0]] = low
                powers[others[1]] = high
                axes = tuple(sorted([axis] + [m for m in others if powers[m]]))
                number = {(0,): 0, (1,): 1, (2,): 2, (0, 1): 3, (0, 2): 4, (1, 2): 5, (0, 1, 2): 6}[axes]
                piece = signs[number] * moment(part[powers[0] * 2 + powers[1]], powers[2])
                total = piece if total is None else total + piece
        return total

    mom = [[mom_ref[s * 4 + i, rows, :] for i in range(4)] for s in range(6)]
    inner = [
        square[0] * mom[0][i] + square[1] * mom[1][i] + square[2] * mom[2][i] for i in range(4)
    ]
    between = {(0, 1): 3, (0, 2): 4, (1, 2): 5}
    for c in range(3):
        part = [inner[i] - (2.0 * square[c]) * mom[c][i] for i in range(4)]
        total = along(c, part)
        for j in range(3):
            if j != c:
                shared = mom[between[(min(c, j), max(c, j))]]
                total = total - square[j] * along(j, shared)
        out_ref[pl.ds(8 * c, 8), :] = total * (factor[c] * live)
    out_ref[pl.ds(24, 8), :] = map_ref[...].astype(jnp.float32)
    spent = live * moment(mom_ref[24, rows, :], 0)
    out_ref[pl.ds(32, 8), :] = jnp.broadcast_to(spent, (8, LANES))


def element_terms(count, velocity, adjoint, spacing, design_map):
    vmem = pl.BlockSpec(memory_space=pltpu.VMEM)
    arrays = (velocity, adjoint, spacing, design_map, jnp.asarray(table()))
    arrays = [pltpu.with_memory_space_constraint(array, pltpu.HBM) for array in arrays]
    return pl.pallas_call(
        terms_kernel,
        out_shape=pltpu.VMEM((SENT, LANES), jnp.float32),
        in_specs=[pl.BlockSpec(memory_space=pltpu.SMEM)]
        + [pl.BlockSpec(memory_space=pltpu.HBM)] * 5,
        out_specs=vmem,
        scratch_shapes=[
            pltpu.VMEM((3, NODES + 9, LANES), jnp.float32),
            pltpu.VMEM((3, NODES + 9, LANES), jnp.float32),
            pltpu.VMEM(spacing.shape, jnp.float32),
            pltpu.VMEM(design_map.shape, jnp.int32),
            pltpu.VMEM((TABLE_ROWS, LANES), jnp.float32),
            pltpu.VMEM((6, P_SIZE, P_SIZE, 8, LANES), jnp.float32),
            pltpu.VMEM((6, P_SIZE, 8, LANES), jnp.float32),
            pltpu.VMEM((6 * P_SIZE * PITCH + 16, LANES), jnp.float32),
            pltpu.VMEM((25, 8, LANES), jnp.float32),
            pltpu.SemaphoreType.DMA((9,)),
        ],
        compiler_params=pltpu.CompilerParams(vmem_limit_bytes=16 * 1024 * 1024),
    )(count, *arrays)


def spread_kernel(groups, columns, count, column_ref, *refs):
    sources = refs[:count]
    adds = len(refs) > count + 3
    base_ref = refs[count]
    sum_ref, left_ref, right_ref = refs[-3:]
    column = column_ref[0]
    per_owner = ND_DEV // WIDE
    high = groups * per_owner
    half = jnp.bfloat16
    tile = (16, LANES)

    def rows_from(count):
        ramp = lax.broadcasted_iota(jnp.int32, (count, LANES), 0).astype(jnp.float32)
        return ramp.astype(half).reshape(count // 16, *tile)

    def spread_row(rows, k):
        return jnp.broadcast_to(rows[k : k + 1], tile).astype(half)[None]

    ramp_wide = rows_from(WIDE)
    ramp_high = rows_from(high)
    one = jnp.ones((), half)
    zero = jnp.zeros((), half)
    for s, source in enumerate(sources):
        node = source[pl.ds(24, 8), :].astype(jnp.int32)
        owner = node >> log2(ND_DEV)
        at = (owner >> log2(columns)) * per_owner + ((node & (ND_DEV - 1)) >> log2(WIDE))
        at = jnp.where((owner & (columns - 1)) == column, at, -1).astype(jnp.float32)
        low = (node & (WIDE - 1)).astype(jnp.float32)
        parts = []
        for c in range(3):
            value = source[pl.ds(8 * c, 8), :]
            coarse = value.astype(half).astype(jnp.float32)
            parts.append((coarse, value - coarse))
        for k in range(8):
            lanes = pl.ds((8 * s + k) * LANES, LANES)
            mask = jnp.where(ramp_wide == spread_row(low, k), one, zero)
            right_ref[:, lanes] = mask.reshape(WIDE, LANES)
            hit = ramp_high == spread_row(at, k)
            for c in range(3):
                for piece in range(2):
                    placed = jnp.where(hit, spread_row(parts[c][piece], k), zero)
                    left_ref[pl.ds((piece * 3 + c) * high, high), lanes] = placed.reshape(high, LANES)
    both = lax.dot_general(
        left_ref[...],
        right_ref[...],
        (((1,), (1,)), ((), ())),
        preferred_element_type=jnp.float32,
    )
    total = both[: 3 * high] + both[3 * high :]
    rest = pl.ds(3 * high, 8)
    if adds:
        sum_ref[pl.ds(0, 3 * high), :] = base_ref[pl.ds(0, 3 * high), :] + total
        sum_ref[rest, :] = base_ref[rest, :]
    else:
        sum_ref[pl.ds(0, 3 * high), :] = total
        sum_ref[rest, 0:LANES] = sources[0][pl.ds(32, 8), :]


def spread(column, sources, base, groups, columns):
    count = len(sources)
    high = groups * (ND_DEV // WIDE)
    vmem = pl.BlockSpec(memory_space=pltpu.VMEM)
    bases = () if base is None else (base,)
    return pl.pallas_call(
        functools.partial(spread_kernel, groups, columns, count),
        out_shape=jax.ShapeDtypeStruct((3 * high + 8, WIDE), jnp.float32),
        in_specs=[pl.BlockSpec(memory_space=pltpu.SMEM)] + [vmem] * (count + len(bases)),
        out_specs=vmem,
        scratch_shapes=[
            pltpu.VMEM((6 * high, count * 8 * LANES), jnp.bfloat16),
            pltpu.VMEM((WIDE, count * 8 * LANES), jnp.bfloat16),
        ],
        cost_estimate=pl.CostEstimate(
            flops=12 * high * count * 8 * LANES * WIDE, bytes_accessed=2000000, transcendentals=0
        ),
        compiler_params=pltpu.CompilerParams(vmem_limit_bytes=16 * 1024 * 1024),
    )(column, *sources, *bases)


def total_kernel(groups, group_ref, *refs):
    partials = refs[:groups]
    grad_ref, part_ref, sum_ref = refs[groups:]
    per_owner = ND_DEV // WIDE
    high = groups * per_owner
    total = partials[0][...]
    for partial in partials[1:]:
        total = total + partial[...]
    sum_ref[...] = total
    design = total[: 3 * high]
    squares = jnp.sum(design * design)
    spent = jnp.sum(total[3 * high : 3 * high + 1])
    lane = lax.broadcasted_iota(jnp.int32, (1, LANES), 1)
    stats = jnp.where(lane == 0, squares, jnp.where(lane == 1, spent, 0.0))
    part_ref[...] = jnp.broadcast_to(stats[None], part_ref.shape)
    for c in range(3):
        start = pl.multiple_of(c * high + group_ref[0] * per_owner, per_owner)
        block = sum_ref[pl.ds(start, per_owner), :]
        for i in range(per_owner):
            grad_ref[c : c + 1, i * WIDE : (i + 1) * WIDE] = block[i : i + 1, :]


def totalled(group, partials, columns):
    groups = len(partials)
    vmem = pl.BlockSpec(memory_space=pltpu.VMEM)
    return pl.pallas_call(
        functools.partial(total_kernel, groups),
        out_shape=(
            jax.ShapeDtypeStruct((3, ND_DEV), jnp.float32),
            jax.ShapeDtypeStruct((columns, 1, LANES), jnp.float32),
        ),
        in_specs=[pl.BlockSpec(memory_space=pltpu.SMEM)] + [vmem] * groups,
        out_specs=(vmem, vmem),
        scratch_shapes=[pltpu.VMEM(partials[0].shape, jnp.float32)],
        compiler_params=pltpu.CompilerParams(vmem_limit_bytes=4 * 1024 * 1024),
    )(group, *partials)


def scale_kernel(over_nodes, over_elements, grad_ref, part_ref, out_ref, objective_ref):
    total = jnp.sum(part_ref[:, 0, :], axis=0, keepdims=True)
    lane = lax.broadcasted_iota(jnp.int32, (1, LANES), 1)
    squares = jnp.sum(jnp.where(lane == 0, total, 0.0), axis=1, keepdims=True)
    spent = jnp.sum(jnp.where(lane == 1, total, 0.0), axis=1, keepdims=True)
    out_ref[...] = grad_ref[...] * lax.rsqrt(squares * over_nodes + 1e-06)
    objective_ref[...] = spent * over_elements


def scaled(grad, parts, over_nodes, over_elements):
    vmem = pl.BlockSpec(memory_space=pltpu.VMEM)
    return pl.pallas_call(
        functools.partial(scale_kernel, over_nodes, over_elements),
        out_shape=(
            jax.ShapeDtypeStruct((3, ND_DEV), jnp.float32),
            jax.ShapeDtypeStruct((1, 1), jnp.float32),
        ),
        in_specs=[vmem, vmem],
        out_specs=(vmem, vmem),
        compiler_params=pltpu.CompilerParams(vmem_limit_bytes=2 * 1024 * 1024),
    )(grad, parts)


def body(velocity, adjoint, spacing, elem_count, design_map):
    slots = velocity.shape[-1]
    groups = lax.axis_size("grp")
    columns = lax.axis_size(ELEM)
    group = lax.axis_index("grp").astype(jnp.int32).reshape(1)
    column = lax.axis_index(ELEM).astype(jnp.int32).reshape(1)
    sent = element_terms(elem_count, velocity, adjoint, spacing, design_map)
    partner = [(e + 1) % columns if e % 2 else (e - 1) % columns for e in range(columns)]
    within = lax.ppermute(sent, "elem_2", [(0, 1), (1, 0)])
    across = lax.ppermute(sent, ELEM, list(enumerate(partner)))
    partial = spread(column, (sent,), None, groups, columns)
    partial = spread(column, (within, across), partial, groups, columns)
    partials = [partial] + [
        lax.ppermute(partial, "grp", [(i, i ^ by) for i in range(groups)]) for by in (1, 3, 2)
    ]
    grad, parts = totalled(group, partials, columns)
    parts = lax.all_to_all(parts, ELEM, split_axis=0, concat_axis=0, tiled=True)
    devices = groups * columns
    direction, objective = scaled(
        grad,
        parts,
        1.0 / (3.0 * ND_DEV * devices),
        1.0 / (NODES * slots * devices),
    )
    return (direction, objective.reshape(()))


def solution(mesh):
    finer = Mesh(
        mesh.devices.reshape(mesh.shape["grp"], 4, 4, 2), ("grp", "elem_0", "elem_1", "elem_2")
    )
    in_specs = (
        P(None, None, GRP_ELEM),
        P(None, None, GRP_ELEM),
        P(None, GRP_ELEM),
        P(GRP_ELEM),
        P(None, GRP_ELEM),
    )
    out_specs = (P(None, GRP_ELEM), P())
    return jax.shard_map(body, mesh=finer, in_specs=in_specs, out_specs=out_specs, check_vma=False)
```

```python
import functools

import jax
import jax.numpy as jnp
import numpy as np
from jax import lax
from jax.experimental import pallas as pl
from jax.experimental.pallas import tpu as pltpu
from jax.sharding import Mesh
from jax.sharding import PartitionSpec as P

P_SIZE = 7
NODES = P_SIZE**3
ND_DEV = 2048
LANES = 128
ELEM = ("elem_0", "elem_1", "elem_2")
GRP_ELEM = ("grp", "elem_0", "elem_1", "elem_2")
SENT = 40
WIDE = 128
UNROLL = 7
PITCH = 9


def log2(number):
    assert number & (number - 1) == 0
    return number.bit_length() - 1


def lobatto(degree):
    points = np.cos(np.pi * np.arange(degree + 1) / degree)
    for sweep in range(60):
        lower = np.ones(degree + 1)
        upper = points.copy()
        for order in range(2, degree + 1):
            lower, upper = (upper, ((2 * order - 1) * points * upper - (order - 1) * lower) / order)
        points = points - (points * upper - lower) / ((degree + 1) * upper)
    lower = np.ones(degree + 1)
    upper = points.copy()
    for order in range(2, degree + 1):
        lower, upper = (upper, ((2 * order - 1) * points * upper - (order - 1) * lower) / order)
    return (points[::-1].copy(), upper[::-1].copy())


def one_dimensional():
    degree = P_SIZE - 1
    points, values = lobatto(degree)
    weights = 2.0 / (degree * (degree + 1) * values**2)
    derivative = np.zeros((P_SIZE, P_SIZE))
    for i in range(P_SIZE):
        for j in range(P_SIZE):
            if i != j:
                derivative[i, j] = values[i] / (values[j] * (points[i] - points[j]))
    derivative[0, 0] = -degree * (degree + 1) / 4.0
    derivative[degree, degree] = degree * (degree + 1) / 4.0
    points[degree // 2] = 0.0
    derivative[degree // 2, degree // 2] = 0.0
    return (points, weights, derivative)


POINTS, WEIGHTS, DERIVATIVE = one_dimensional()
ACROSS, ALONG, SIGNS = 0, 16, 32
TABLE_ROWS = 88


def table():
    rows = np.zeros((TABLE_ROWS, LANES), np.float32)
    rows[ACROSS : ACROSS + P_SIZE] = WEIGHTS[:, None]
    rows[ACROSS + 8 : ACROSS + 8 + P_SIZE] = (WEIGHTS * POINTS)[:, None]
    rows[ALONG : ALONG + P_SIZE] = WEIGHTS[:, None]
    rows[ALONG + 8 : ALONG + 8 + P_SIZE] = (WEIGHTS * POINTS)[:, None]
    for number, axes in enumerate(((0,), (1,), (2,), (0, 1), (0, 2), (1, 2), (0, 1, 2))):
        for vertex in range(8):
            sign = np.prod([2.0 * (vertex >> 2 - m & 1) - 1.0 for m in axes])
            rows[SIGNS + 8 * number + vertex] = sign / 8.0
    return rows


def along_vectors(f):
    half = P_SIZE // 2
    last = P_SIZE - 1
    even = [f[j] + f[last - j] for j in range(half)]
    odd = [f[j] - f[last - j] for j in range(half)]
    out = [None] * P_SIZE
    for i in range(half + 1):
        coef = DERIVATIVE[i]
        b = None
        for j in range(half):
            piece = float((coef[j] - coef[last - j]) / 2) * odd[j]
            b = piece if b is None else b + piece
        if i == half:
            out[i] = b
            continue
        a = float(coef[half]) * f[half]
        for j in range(half):
            a = a + float((coef[j] + coef[last - j]) / 2) * even[j]
        out[i] = b + a
        out[last - i] = b - a
    return out


def terms_kernel(
    count_ref,
    u_hbm,
    w_hbm,
    h_hbm,
    map_hbm,
    tab_hbm,
    out_ref,
    u_ref,
    w_ref,
    h_ref,
    map_ref,
    tab_ref,
    ga_ref,
    gb_ref,
    gc_ref,
    mom_ref,
    sems,
):
    n = P_SIZE
    fields = [(ref, i) for ref in (u_ref, w_ref) for i in range(3)]
    rows = pl.ds(0, n)
    whole = pl.ds(0, NODES)
    pairs = [
        (source.at[i], ref.at[i, whole])
        for source, ref in ((u_hbm, u_ref), (w_hbm, w_ref))
        for i in range(3)
    ]
    pairs += [(tab_hbm, tab_ref), (h_hbm, h_ref), (map_hbm, map_ref)]
    copies = [
        pltpu.make_async_copy(source, target, sems.at[i])
        for i, (source, target) in enumerate(pairs)
    ]
    for copy in copies:
        copy.start()

    def first(f, ref, i, b):
        slabs = [ref[i, pl.ds(a * n * n + b * n, n), :] for a in range(n)]
        for a, value in enumerate(along_vectors(slabs)):
            ga_ref[f, a, b, rows, :] = value

    mom_ref[...] = jnp.zeros_like(mom_ref)
    for f, (ref, i) in enumerate(fields):
        copies[f].wait()

        def step(b, carry, f=f, ref=ref, i=i):
            first(f, ref, i, b)
            return carry

        lax.fori_loop(0, n, step, 0, unroll=UNROLL)
    for copy in copies[6:]:
        copy.wait()

    h = h_ref[...]
    factor = [2.0 / h[j : j + 1] for j in range(3)]
    square = [f * f for f in factor]

    def second(a, carry):
        base = a * n * n
        for f, (ref, i) in enumerate(fields):
            slabs = [ref[i, pl.ds(base + b * n, n), :] for b in range(n)]
            for b, value in enumerate(along_vectors(slabs)):
                gb_ref[f, b, rows, :] = value
            slabs = [ref[i, pl.ds(base + c, n, stride=n), :] for c in range(n)]
            for c, value in enumerate(along_vectors(slabs)):
                gc_ref[pl.ds((f * n + c) * PITCH, n), :] = value
        sums = [[None, None] for _ in range(6)]
        kept = [None] * 6
        spent = None
        for b in [0, 6, 1, 5, 2, 4, 3]:
            grads = []
            for f in range(6):
                gc = gc_ref[pl.ds(f * n * PITCH + b, n, stride=PITCH), :]
                grads.append([ga_ref[f, a, b, rows, :], gb_ref[f, b, rows, :], gc])
            gu, gw = grads[:3], grads[3:]

            def cross(c, j):
                return gu[0][c] * gw[0][j] + gu[1][c] * gw[1][j] + gu[2][c] * gw[2][j]

            pairs = [cross(0, 0), cross(1, 1), cross(2, 2)]
            pairs += [cross(c, j) + cross(j, c) for c, j in ((0, 1), (0, 2), (1, 2))]
            own = [gu[0][j] * gu[0][j] + gu[1][j] * gu[1][j] + gu[2][j] * gu[2][j] for j in range(3)]
            squared = own[0] * square[0] + own[1] * square[1] + own[2] * square[2]
            for s, value in enumerate(pairs):
                if b < n // 2:
                    kept[s] = value
                    continue
                if b == n // 2:
                    sums[s][0] = sums[s][0] + float(WEIGHTS[b]) * value
                    continue
                total = float(WEIGHTS[b]) * (value + kept[s])
                slope = float(WEIGHTS[b] * POINTS[b]) * (value - kept[s])
                sums[s][0] = total if sums[s][0] is None else sums[s][0] + total
                sums[s][1] = slope if sums[s][1] is None else sums[s][1] + slope
            piece = float(WEIGHTS[b]) * squared
            spent = piece if spent is None else spent + piece
        wa = tab_ref[pl.ds(ALONG + a, 1), :]
        wxa = tab_ref[pl.ds(ALONG + 8 + a, 1), :]
        for s in range(6):
            for r, scale in enumerate((wa, wxa)):
                for t in range(2):
                    at = s * 4 + r * 2 + t
                    mom_ref[at, rows, :] = mom_ref[at, rows, :] + scale * sums[s][t]
        mom_ref[24, rows, :] = mom_ref[24, rows, :] + wa * spent
        return carry

    lax.fori_loop(0, n, second, 0, unroll=n)

    jacobian = h[0:1] * h[1:2] * h[2:3] * 0.125
    lanes = lax.broadcasted_iota(jnp.int32, (1, LANES), 1)
    live = jacobian * (lanes < count_ref[0]).astype(jnp.float32)
    flat = tab_ref[pl.ds(ACROSS, n), :]
    slant = tab_ref[pl.ds(ACROSS + 8, n), :]
    signs = [tab_ref[pl.ds(SIGNS + 8 * i, 8), :] for i in range(7)]

    def moment(value, c):
        return jnp.sum(value * (slant if c else flat), axis=0, keepdims=True)

    def along(axis, part):
        others = [m for m in range(3) if m != axis]
        total = None
        for low in range(2):
            for high in range(2):
                powers = [0, 0, 0]
                powers[others[0]] = low
                powers[others[1]] = high
                axes = tuple(sorted([axis] + [m for m in others if powers[m]]))
                number = {(0,): 0, (1,): 1, (2,): 2, (0, 1): 3, (0, 2): 4, (1, 2): 5, (0, 1, 2): 6}[axes]
                piece = signs[number] * moment(part[powers[0] * 2 + powers[1]], powers[2])
                total = piece if total is None else total + piece
        return total

    mom = [[mom_ref[s * 4 + i, rows, :] for i in range(4)] for s in range(6)]
    inner = [
        square[0] * mom[0][i] + square[1] * mom[1][i] + square[2] * mom[2][i] for i in range(4)
    ]
    between = {(0, 1): 3, (0, 2): 4, (1, 2): 5}
    for c in range(3):
        part = [inner[i] - (2.0 * square[c]) * mom[c][i] for i in range(4)]
        total = along(c, part)
        for j in range(3):
            if j != c:
                shared = mom[between[(min(c, j), max(c, j))]]
                total = total - square[j] * along(j, shared)
        out_ref[pl.ds(8 * c, 8), :] = total * (factor[c] * live)
    out_ref[pl.ds(24, 8), :] = map_ref[...].astype(jnp.float32)
    spent = live * moment(mom_ref[24, rows, :], 0)
    out_ref[pl.ds(32, 8), :] = jnp.broadcast_to(spent, (8, LANES))


def element_terms(count, velocity, adjoint, spacing, design_map):
    vmem = pl.BlockSpec(memory_space=pltpu.VMEM)
    arrays = (velocity, adjoint, spacing, design_map, jnp.asarray(table()))
    arrays = [pltpu.with_memory_space_constraint(array, pltpu.HBM) for array in arrays]
    return pl.pallas_call(
        terms_kernel,
        out_shape=pltpu.VMEM((SENT, LANES), jnp.float32),
        in_specs=[pl.BlockSpec(memory_space=pltpu.SMEM)]
        + [pl.BlockSpec(memory_space=pltpu.HBM)] * 5,
        out_specs=vmem,
        scratch_shapes=[
            pltpu.VMEM((3, NODES + 9, LANES), jnp.float32),
            pltpu.VMEM((3, NODES + 9, LANES), jnp.float32),
            pltpu.VMEM(spacing.shape, jnp.float32),
            pltpu.VMEM(design_map.shape, jnp.int32),
            pltpu.VMEM((TABLE_ROWS, LANES), jnp.float32),
            pltpu.VMEM((6, P_SIZE, P_SIZE, 8, LANES), jnp.float32),
            pltpu.VMEM((6, P_SIZE, 8, LANES), jnp.float32),
            pltpu.VMEM((6 * P_SIZE * PITCH + 16, LANES), jnp.float32),
            pltpu.VMEM((25, 8, LANES), jnp.float32),
            pltpu.SemaphoreType.DMA((9,)),
        ],
        compiler_params=pltpu.CompilerParams(vmem_limit_bytes=16 * 1024 * 1024),
    )(count, *arrays)


def spread_kernel(groups, columns, count, column_ref, *refs):
    sources = refs[:count]
    adds = len(refs) > count + 3
    base_ref = refs[count]
    sum_ref, left_ref, right_ref = refs[-3:]
    column = column_ref[0]
    per_owner = ND_DEV // WIDE
    high = groups * per_owner
    half = jnp.bfloat16
    tile = (16, LANES)

    def rows_from(count):
        ramp = lax.broadcasted_iota(jnp.int32, (count, LANES), 0).astype(jnp.float32)
        return ramp.astype(half).reshape(count // 16, *tile)

    def spread_row(rows, k):
        return jnp.broadcast_to(rows[k : k + 1], tile).astype(half)[None]

    ramp_wide = rows_from(WIDE)
    ramp_high = rows_from(high)
    one = jnp.ones((), half)
    zero = jnp.zeros((), half)
    for s, source in enumerate(sources):
        node = source[pl.ds(24, 8), :].astype(jnp.int32)
        owner = node >> log2(ND_DEV)
        at = (owner >> log2(columns)) * per_owner + ((node & (ND_DEV - 1)) >> log2(WIDE))
        at = jnp.where((owner & (columns - 1)) == column, at, -1).astype(jnp.float32)
        low = (node & (WIDE - 1)).astype(jnp.float32)
        parts = []
        for c in range(3):
            value = source[pl.ds(8 * c, 8), :]
            coarse = value.astype(half).astype(jnp.float32)
            parts.append((coarse, value - coarse))
        for k in range(8):
            lanes = pl.ds((8 * s + k) * LANES, LANES)
            mask = jnp.where(ramp_wide == spread_row(low, k), one, zero)
            right_ref[:, lanes] = mask.reshape(WIDE, LANES)
            hit = ramp_high == spread_row(at, k)
            for c in range(3):
                for piece in range(2):
                    placed = jnp.where(hit, spread_row(parts[c][piece], k), zero)
                    left_ref[pl.ds((piece * 3 + c) * high, high), lanes] = placed.reshape(high, LANES)
    both = lax.dot_general(
        left_ref[...],
        right_ref[...],
        (((1,), (1,)), ((), ())),
        preferred_element_type=jnp.float32,
    )
    total = both[: 3 * high] + both[3 * high :]
    rest = pl.ds(3 * high, 8)
    if adds:
        sum_ref[pl.ds(0, 3 * high), :] = base_ref[pl.ds(0, 3 * high), :] + total
        sum_ref[rest, :] = base_ref[rest, :]
    else:
        sum_ref[pl.ds(0, 3 * high), :] = total
        sum_ref[rest, 0:LANES] = sources[0][pl.ds(32, 8), :]


def spread(column, sources, base, groups, columns):
    count = len(sources)
    high = groups * (ND_DEV // WIDE)
    vmem = pl.BlockSpec(memory_space=pltpu.VMEM)
    bases = () if base is None else (base,)
    return pl.pallas_call(
        functools.partial(spread_kernel, groups, columns, count),
        out_shape=jax.ShapeDtypeStruct((3 * high + 8, WIDE), jnp.float32),
        in_specs=[pl.BlockSpec(memory_space=pltpu.SMEM)] + [vmem] * (count + len(bases)),
        out_specs=vmem,
        scratch_shapes=[
            pltpu.VMEM((6 * high, count * 8 * LANES), jnp.bfloat16),
            pltpu.VMEM((WIDE, count * 8 * LANES), jnp.bfloat16),
        ],
        cost_estimate=pl.CostEstimate(
            flops=12 * high * count * 8 * LANES * WIDE, bytes_accessed=2000000, transcendentals=0
        ),
        compiler_params=pltpu.CompilerParams(vmem_limit_bytes=16 * 1024 * 1024),
    )(column, *sources, *bases)


def total_kernel(groups, group_ref, *refs):
    partials = refs[:groups]
    grad_ref, part_ref, sum_ref = refs[groups:]
    per_owner = ND_DEV // WIDE
    high = groups * per_owner
    total = partials[0][...]
    for partial in partials[1:]:
        total = total + partial[...]
    sum_ref[...] = total
    design = total[: 3 * high]
    squares = jnp.sum(design * design)
    spent = jnp.sum(total[3 * high : 3 * high + 1])
    lane = lax.broadcasted_iota(jnp.int32, (1, LANES), 1)
    stats = jnp.where(lane == 0, squares, jnp.where(lane == 1, spent, 0.0))
    part_ref[...] = jnp.broadcast_to(stats[None], part_ref.shape)
    for c in range(3):
        start = pl.multiple_of(c * high + group_ref[0] * per_owner, per_owner)
        block = sum_ref[pl.ds(start, per_owner), :]
        for i in range(per_owner):
            grad_ref[c : c + 1, i * WIDE : (i + 1) * WIDE] = block[i : i + 1, :]


def totalled(group, partials, columns):
    groups = len(partials)
    vmem = pl.BlockSpec(memory_space=pltpu.VMEM)
    return pl.pallas_call(
        functools.partial(total_kernel, groups),
        out_shape=(
            jax.ShapeDtypeStruct((3, ND_DEV), jnp.float32),
            jax.ShapeDtypeStruct((columns, 1, LANES), jnp.float32),
        ),
        in_specs=[pl.BlockSpec(memory_space=pltpu.SMEM)] + [vmem] * groups,
        out_specs=(vmem, vmem),
        scratch_shapes=[pltpu.VMEM(partials[0].shape, jnp.float32)],
        compiler_params=pltpu.CompilerParams(vmem_limit_bytes=4 * 1024 * 1024),
    )(group, *partials)


def scale_kernel(over_nodes, over_elements, grad_ref, part_ref, out_ref, objective_ref):
    total = jnp.sum(part_ref[:, 0, :], axis=0, keepdims=True)
    lane = lax.broadcasted_iota(jnp.int32, (1, LANES), 1)
    squares = jnp.sum(jnp.where(lane == 0, total, 0.0), axis=1, keepdims=True)
    spent = jnp.sum(jnp.where(lane == 1, total, 0.0), axis=1, keepdims=True)
    out_ref[...] = grad_ref[...] * lax.rsqrt(squares * over_nodes + 1e-06)
    objective_ref[...] = spent * over_elements


def scaled(grad, parts, over_nodes, over_elements):
    vmem = pl.BlockSpec(memory_space=pltpu.VMEM)
    return pl.pallas_call(
        functools.partial(scale_kernel, over_nodes, over_elements),
        out_shape=(
            jax.ShapeDtypeStruct((3, ND_DEV), jnp.float32),
            jax.ShapeDtypeStruct((1, 1), jnp.float32),
        ),
        in_specs=[vmem, vmem],
        out_specs=(vmem, vmem),
        compiler_params=pltpu.CompilerParams(vmem_limit_bytes=2 * 1024 * 1024),
    )(grad, parts)


def body(velocity, adjoint, spacing, elem_count, design_map):
    slots = velocity.shape[-1]
    groups = lax.axis_size("grp")
    columns = lax.axis_size(ELEM)
    group = lax.axis_index("grp").astype(jnp.int32).reshape(1)
    column = lax.axis_index(ELEM).astype(jnp.int32).reshape(1)
    sent = element_terms(elem_count, velocity, adjoint, spacing, design_map)
    partner = [(e + 1) % columns if e % 2 else (e - 1) % columns for e in range(columns)]
    within = lax.ppermute(sent, "elem_2", [(0, 1), (1, 0)])
    across = lax.ppermute(sent, ELEM, list(enumerate(partner)))
    partial = spread(column, (sent,), None, groups, columns)
    partial = spread(column, (within, across), partial, groups, columns)
    partials = [partial] + [
        lax.ppermute(partial, "grp", [(i, i ^ by) for i in range(groups)]) for by in (1, 3, 2)
    ]
    grad, parts = totalled(group, partials, columns)
    parts = lax.all_to_all(parts, ELEM, split_axis=0, concat_axis=0, tiled=True)
    devices = groups * columns
    direction, objective = scaled(
        grad,
        parts,
        1.0 / (3.0 * ND_DEV * devices),
        1.0 / (NODES * slots * devices),
    )
    return (direction, objective.reshape(()))


def solution(mesh):
    finer = Mesh(
        mesh.devices.reshape(mesh.shape["grp"], 4, 4, 2), ("grp", "elem_0", "elem_1", "elem_2")
    )
    in_specs = (
        P(None, None, GRP_ELEM),
        P(None, None, GRP_ELEM),
        P(None, GRP_ELEM),
        P(GRP_ELEM),
        P(None, GRP_ELEM),
    )
    out_specs = (P(None, GRP_ELEM), P())
    return jax.shard_map(body, mesh=finer, in_specs=in_specs, out_specs=out_specs, check_vma=False)
```
